32 devices in a mesh: rows: 2 (over y), cols: 16 (over z, x, core).
Axes of the slice: x: 2, y: 2, z: 4, core: 2. Of those that a mesh axis runs over, the one named last changes fastest.
Arguments:
- covariance: float32 [2048, 2048], P('rows', 'cols'), may hold values from -6 to 6
- zonal: float32 [16, 128, 128], P('rows'), may hold values from -0.5 to 0.5
- stencil: float32 [16, 3, 128], P('rows'), may hold values from -0.5 to 1.1, as said below
Outputs:
- lagged: float32 [2048, 2048], P('rows', 'cols')
The draws below stay inside these ranges and needn't reach their ends.
Inputs may be any that keep to these rules, and one draw needn't show every extreme that they name: `stencil`: component 0 lies in 0.7 to 1.1, components 1 and 2 in -0.5 to 0.5.
All inputs are finite; a program needn't handle non-finite values.
Results may differ from the reference program's by a relative error of at most 0.0003.
Values sent between devices are 32-bit elements; how exact they have to be, the bound alone decides.
No kernel may reach another device: no remote copies, remote signals or barrier semaphores. Data moves between devices by JAX's collectives and lax.ppermute only.
A program may use at most 64 MiB of HBM per device.

```python
import jax
import jax.numpy as jnp
from jax import lax

LON = 128
STEPS = 3
LAGS = 3
NLAT = 16
NSTATE = 2048


def draw_stencil(key, part):
    first, second = jax.random.split(jax.random.fold_in(key, 11))
    middle = jax.random.uniform(first, (NLAT, 1, LON), jnp.float32, 0.7, 1.1)
    sides = jax.random.uniform(second, (NLAT, 2, LON), jnp.float32, -0.5, 0.5)
    return jnp.concatenate([middle, sides], axis=1)


def level_of(rng, extent, cuts, low, largest):
    level = 1.0
    for dim, shards_of in cuts:
        steps = jax.random.uniform(jax.random.fold_in(jax.random.fold_in(rng, 6), dim), (shards_of,), jnp.float32, low / len(cuts), largest / len(cuts))
        level = level * jnp.repeat(jnp.exp(steps), extent[dim] // shards_of).reshape((-1,) + (1,) * (len(extent) - 1 - dim))
    return level


def scatter_about(own_key, extent, deviation, reach, cuts=(), held_as=jnp.bfloat16):
    result = deviation * jax.random.normal(own_key, extent, jnp.float32)
    if cuts:
        result = result * level_of(own_key, extent, cuts, -0.22, 0.18)
    return jnp.clip(result, -reach, reach).astype(held_as)


def setup_inputs(seed: int = 0) -> dict:
    splits = jax.random.split(jax.random.key(seed), 4)
    covariance = scatter_about(splits[0], (NSTATE, NSTATE), 1.0, 6.0, ((0, 2), (1, 16)), jnp.float32)
    zonal = scatter_about(splits[1], (NLAT, LON, LON), LON ** -0.5, 0.5, ((0, 2),), jnp.float32)
    stencil = draw_stencil(jax.random.fold_in(splits[3], 71), 0)
    return {"covariance": covariance, "zonal": zonal, "stencil": stencil}


def left_apply(matrix, zonal, stencil):
    latitudes = zonal.shape[0]
    longitudes = zonal.shape[1]
    blocks = matrix.reshape(latitudes, longitudes, matrix.shape[1])

    def one_latitude(lat):
        north_lat = jnp.minimum(lat + 1, latitudes - 1).astype(jnp.int32)
        south_lat = jnp.maximum(lat - 1, 0).astype(jnp.int32)
        north_flag = jnp.where(lat + 1 < latitudes, 1.0, 0.0).astype(matrix.dtype)
        south_flag = jnp.where(lat > 0, 1.0, 0.0).astype(matrix.dtype)
        own = lax.dynamic_index_in_dim(blocks, lat, 0, False)
        north = lax.dynamic_index_in_dim(blocks, north_lat, 0, False) * north_flag
        south = lax.dynamic_index_in_dim(blocks, south_lat, 0, False) * south_flag
        coeffs = lax.dynamic_index_in_dim(stencil, lat, 0, False)
        mixed = coeffs[0][:, None] * own + coeffs[1][:, None] * north + coeffs[2][:, None] * south
        matrix_lat = lax.dynamic_index_in_dim(zonal, lat, 0, False)
        return jnp.dot(matrix_lat, mixed, preferred_element_type=jnp.float32, precision=lax.Precision.HIGHEST).astype(matrix.dtype)

    turned = lax.map(one_latitude, jnp.arange(latitudes, dtype=jnp.int32))
    return turned.reshape(matrix.shape)


def reference(covariance, zonal, stencil):
    current = covariance
    for repeat in range(STEPS):
        current = left_apply(current, zonal, stencil)
    current = current.T
    for repeat in range(STEPS):
        current = left_apply(current, zonal, stencil)
    for repeat in range(LAGS):
        current = left_apply(current, zonal, stencil)
    return current
```

```python
import functools

import jax
import jax.numpy as jnp
from jax import lax
from jax.experimental import pallas as pl
from jax.experimental.pallas import tpu as pltpu
from jax.sharding import PartitionSpec as P

STEPS = 3
LAGS = 3
VMEM = pl.BlockSpec(memory_space=pltpu.VMEM)
PARAMS = pltpu.CompilerParams(vmem_limit_bytes=48 * 1024 * 1024)
NT = (((1,), (1,)), ((), ()))


def split(value):
    high = value.astype(jnp.bfloat16)
    low = (value - high.astype(jnp.float32)).astype(jnp.bfloat16)
    return high, low


def prepare_operators(zonal_of, lats, ops):
    for lat in range(lats):
        high, low = split(zonal_of(lat))
        ops[lat] = jnp.concatenate([high, high, low], axis=1)


def apply_steps(state, ops, weights, lats, count):
    def one(step, carry):
        before = None
        own = state[0]
        for lat in range(lats):
            after = state[lat + 1] if lat + 1 < lats else None
            mixed = weights[lat, 0:1, :] * own
            if after is not None:
                mixed = mixed + weights[lat, 1:2, :] * after
            if before is not None:
                mixed = mixed + weights[lat, 2:3, :] * before
            high, low = split(mixed)
            state[lat] = lax.dot_general(
                jnp.concatenate([high, low, high], axis=1),
                ops[lat],
                NT,
                preferred_element_type=jnp.float32,
            )
            before, own = own, after
        return carry

    lax.fori_loop(0, count, one, 0)


def cut_kernel(pieces, share, block, zonal, stencil, *outs):
    me = lax.axis_index("rows")
    core = lax.axis_index("cols") % share
    width = block.shape[1] // pieces
    tall = block.shape[0]
    lons = zonal.shape[1]
    for partner in range(pieces):
        target = me ^ partner
        for first in range(0, tall, lons):
            turned = block[first : first + lons, :].T
            for other in range(pieces):

                @pl.when(target == other)
                def _():
                    outs[partner][:, first : first + lons] = turned[other * width : (other + 1) * width]

    packet = outs[pieces]
    count = zonal.shape[0] // share
    for lat in range(count):
        packet[lat * lons : (lat + 1) * lons, :] = zonal[core * count + lat]
        packet[count * lons + 8 * lat : count * lons + 8 * lat + 3, :] = stencil[core * count + lat]


def load_operators(pieces, share, zonal, stencil, packets, ops, weights):
    me = lax.axis_index("rows")
    core = lax.axis_index("cols") % share
    lat_rows, lons = zonal.shape[:2]
    count = lat_rows // share

    def put(lat, matrix, coeffs):
        high, low = split(matrix)
        ops[lat] = jnp.concatenate([high, high, low], axis=1)
        weights[lat, 0:3, :] = coeffs

    for lat in range(lat_rows):
        put(me * lat_rows + lat, zonal[lat], stencil[lat])
    for partner in range(1, pieces):
        for part in range(share):
            packet = packets[(partner - 1) * share + part]
            first = (me ^ partner) * lat_rows + (core ^ part) * count
            for lat in range(count):
                put(
                    first + lat,
                    packet[lat * lons : (lat + 1) * lons, :],
                    packet[count * lons + 8 * lat : count * lons + 8 * lat + 3, :],
                )


def first_kernel(pieces, share, cols, *refs):
    n_packets = (pieces - 1) * share
    blocks = refs[:pieces]
    zonal, stencil = refs[pieces : pieces + 2]
    packets = refs[pieces + 2 : pieces + 2 + n_packets]
    out, state, ops, weights = refs[pieces + 2 + n_packets :]
    me = lax.axis_index("rows")
    lat_rows, lons = zonal.shape[:2]
    lats = pieces * lat_rows
    for partner in range(pieces):
        for lat in range(lat_rows):
            state[(me ^ partner) * lat_rows + lat] = blocks[partner][:, lat * lons : (lat + 1) * lons]
    load_operators(pieces, share, zonal, stencil, packets, ops, weights)
    apply_steps(state, ops, weights, lats, STEPS)
    width = state.shape[1]
    fold = lons // width
    short = width // fold
    for lat in range(lats):
        turned = state[lat].T
        for sub in range(fold):
            index = lat * fold + sub
            target = index % pieces * cols + index // pieces
            out[target] = jnp.concatenate(
                [
                    turned[sub * width + part * short : sub * width + (part + 1) * short]
                    for part in range(fold)
                ],
                axis=1,
            )


def second_kernel(pieces, share, cols, *refs):
    n_packets = (pieces - 1) * share
    moved, zonal, stencil = refs[:3]
    packets = refs[3 : 3 + n_packets]
    outs = refs[3 + n_packets : 3 + n_packets + pieces]
    state, ops, weights = refs[3 + n_packets + pieces :]
    me = lax.axis_index("rows")
    lat_rows, lons = zonal.shape[:2]
    lats = pieces * lat_rows
    width = state.shape[1]
    fold = lons // width
    short = width // fold
    for lat in range(lats):
        got = []
        for sub in range(fold):
            index = lat * fold + sub
            got.append(moved[index % pieces * cols + index // pieces])
        for part in range(fold):
            state[lat, part * short : (part + 1) * short, :] = jnp.concatenate(
                [block[:, part * width : (part + 1) * width] for block in got], axis=1
            )
    load_operators(pieces, share, zonal, stencil, packets, ops, weights)
    apply_steps(state, ops, weights, lats, STEPS + LAGS)
    for partner in range(pieces):
        for lat in range(lat_rows):
            outs[partner][:, lat * lons : (lat + 1) * lons] = state[(me ^ partner) * lat_rows + lat]


def join_kernel(pieces, *refs):
    blocks, out, stack = refs[:pieces], refs[pieces], refs[pieces + 1]
    me = lax.axis_index("rows")
    width, tall = blocks[0].shape
    lons = 128 if tall % 128 == 0 else tall
    for partner in range(pieces):
        stack[me ^ partner] = blocks[partner][...]
    for first in range(0, tall, lons):
        rows = jnp.concatenate([stack[i, :, first : first + lons] for i in range(pieces)], axis=0)
        out[first : first + lons, :] = rows.T


def call(kernel, out_shape, args, scratch=()):
    single = not isinstance(out_shape, (list, tuple))
    return pl.pallas_call(
        kernel,
        out_shape=out_shape,
        in_specs=[VMEM] * len(args),
        out_specs=VMEM if single else [VMEM] * len(out_shape),
        scratch_shapes=list(scratch),
        compiler_params=PARAMS,
    )(*args)


def on_device(covariance, zonal, stencil):
    pieces = lax.axis_size("rows")
    cols = lax.axis_size("cols")
    share = 2
    tall, wide = covariance.shape
    lat_rows, lons = zonal.shape[:2]
    lats = lat_rows * pieces
    width = wide // pieces
    count = lat_rows // share
    f32 = jnp.float32

    def row_swap(value, partner):
        return lax.ppermute(value, "rows", [(i, i ^ partner) for i in range(pieces)])

    def core_swap(value, part):
        return lax.ppermute(value, "cols", [(i, i ^ part) for i in range(cols)])

    strip = jax.ShapeDtypeStruct((width, tall), f32)
    packet_shape = jax.ShapeDtypeStruct((count * (lons + 8), lons), f32)
    cut = call(
        functools.partial(cut_kernel, pieces, share),
        [strip] * pieces + [packet_shape],
        (covariance, zonal, stencil),
    )
    packets = []
    for partner in range(1, pieces):
        direct = row_swap(cut[pieces], partner)
        packets += [direct, core_swap(direct, 1)]
    blocks = [cut[0]] + [row_swap(cut[partner], partner) for partner in range(1, pieces)]
    scratch = [
        pltpu.VMEM((lats, width, lons), f32),
        pltpu.VMEM((lats, lons, 3 * lons), jnp.bfloat16),
        pltpu.VMEM((lats, 8, lons), f32),
    ]
    packed = jax.ShapeDtypeStruct((pieces * cols, width * width // lons, lons), f32)
    sent = call(
        functools.partial(first_kernel, pieces, share, cols),
        packed,
        (*blocks, zonal, stencil, *packets),
        scratch,
    )
    moved = lax.all_to_all(sent, ("rows", "cols"), 0, 0, tiled=True)
    ends = call(
        functools.partial(second_kernel, pieces, share, cols),
        [strip] * pieces,
        (moved, zonal, stencil, *packets),
        scratch,
    )
    blocks = [ends[0]] + [row_swap(ends[partner], partner) for partner in range(1, pieces)]
    return call(
        functools.partial(join_kernel, pieces),
        jax.ShapeDtypeStruct((tall, wide), f32),
        blocks,
        [pltpu.VMEM((pieces, width, tall), f32)],
    )


def solution(mesh):
    placed = (P("rows", "cols"), P("rows", None, None), P("rows", None, None))
    return jax.shard_map(
        on_device, mesh=mesh, in_specs=placed, out_specs=P("rows", "cols"), check_vma=False
    )
```

```python
import functools

import jax
import jax.numpy as jnp
from jax import lax
from jax.experimental import pallas as pl
from jax.experimental.pallas import tpu as pltpu
from jax.sharding import PartitionSpec as P

STEPS = 3
LAGS = 3
VMEM = pl.BlockSpec(memory_space=pltpu.VMEM)
HBM = pl.BlockSpec(memory_space=pltpu.HBM)
LIMIT = 32 * 1024 * 1024
F32 = jnp.float32
BF16 = jnp.bfloat16


def split(value):
    high = value.astype(BF16)
    low = (value - high.astype(F32)).astype(BF16)
    return high, low


def call(kernel, out_shape, args, scratch=(), specs=None, flops=0, moved=0):
    single = not isinstance(out_shape, (list, tuple))
    return pl.pallas_call(
        kernel,
        out_shape=out_shape,
        in_specs=specs or [VMEM] * len(args),
        out_specs=VMEM if single else [VMEM] * len(out_shape),
        scratch_shapes=list(scratch),
        compiler_params=pltpu.CompilerParams(vmem_limit_bytes=LIMIT),
        cost_estimate=pl.CostEstimate(flops=flops, bytes_accessed=moved, transcendentals=0),
    )(*args)


def place(pieces, lats, lat):
    if pieces != 2:
        return lat
    return jnp.where(lax.axis_index("rows") == 0, lats - 1 - lat, lat)


def advance(state, ops, weights, first, last, before):
    lats = state.shape[0]
    own = state[first]
    for at in range(first, last):
        after = state[at + 1] if at + 1 < lats else None
        mixed = weights[at, 0:1, :] * own
        if after is not None:
            mixed = mixed + weights[at, 1:2, :] * after
        if before is not None:
            mixed = mixed + weights[at, 2:3, :] * before
        high, low = split(mixed)
        state[at] = jnp.dot(
            jnp.concatenate([high, low, high], axis=1), ops[at], preferred_element_type=F32
        )
        before, own = own, after
    return before


def packet_kernel(share, zonal, stencil, packet, held, sems):
    part = lax.axis_index("cols") % share
    lat_rows, lons = zonal.shape[:2]
    count = lat_rows // share
    copies = [
        pltpu.make_async_copy(
            zonal.at[part * count + i], packet.at[pl.ds(i * lons, lons)], sems.at[i]
        )
        for i in range(count)
    ]
    copies.append(pltpu.make_async_copy(stencil, held, sems.at[count]))
    for copy in copies:
        copy.start()
    copies[-1].wait()
    for i in range(count):
        for k in range(3):
            row = count * lons + 3 * i + k
            packet[row : row + 1, :] = held[k, pl.ds(part * count + i, 1), :]
    for copy in copies[:-1]:
        copy.wait()


def cut_kernel(pieces, block, packet, *refs):
    outs, held, sems = refs[:pieces], refs[pieces], refs[pieces + 1]
    me = lax.axis_index("rows")
    tall, wide = block.shape
    width = wide // pieces
    chunk = min(tall, 128)
    copies = [
        pltpu.make_async_copy(
            block.at[pl.ds(first, chunk)], held.at[pl.ds(first, chunk)], sems.at[first // chunk]
        )
        for first in range(0, tall, chunk)
    ]
    for copy in copies:
        copy.start()
    for first, copy in zip(range(0, tall, chunk), copies):
        copy.wait()
        turned = held[first : first + chunk, :].T
        for piece in range(pieces):
            for partner in range(pieces):

                @pl.when((me ^ partner) == piece)
                def _():
                    outs[partner][:, first : first + chunk] = turned[piece * width : (piece + 1) * width]


def put(ops, weights, at, flipped, matrix, coeffs):
    high, low = split(matrix.T)
    ops[at] = jnp.concatenate([high, high, low], axis=0)
    own, north, south = coeffs
    weights[at, 0:1, :] = own
    weights[at, 1:2, :] = jnp.where(flipped, south, north)
    weights[at, 2:3, :] = jnp.where(flipped, north, south)


def steps(state, ops, weights, count):
    lats = state.shape[0]

    def one(step, carry):
        advance(state, ops, weights, 0, lats, None)
        return carry

    lax.fori_loop(0, count, one, 0, unroll=lats * count <= 128)


def load_kernel(pieces, *refs):
    blocks = refs[:pieces]
    zonal, stencil, state, ops, weights = refs[pieces:]
    me = lax.axis_index("rows")
    lat_rows, lons = zonal.shape[:2]
    lats = pieces * lat_rows
    flipped = place(pieces, lats, 0) != 0
    for lat in range(lat_rows):
        coeffs = [stencil[k, lat : lat + 1, :] for k in range(3)]
        put(ops, weights, lat, flipped, zonal[lat], coeffs)
    for partner in range(pieces):
        for lat in range(lat_rows):
            at = place(pieces, lats, (me ^ partner) * lat_rows + lat)
            state[at] = blocks[partner][:, lat * lons : (lat + 1) * lons]


def first_kernel(pieces, share, cols, *refs):
    n_packets = (pieces - 1) * share
    packets = refs[:n_packets]
    given, own_ops, own_weights, out, ops, weights, state = refs[n_packets:]
    me = lax.axis_index("rows")
    part = lax.axis_index("cols") % share
    lats, width, lons = given.shape
    lat_rows = lats // pieces
    count = lat_rows // share
    flipped = place(pieces, lats, 0) != 0
    for partner in range(1, pieces):
        for other in range(share):
            packet = packets[(partner - 1) * share + other]
            first = (me ^ partner) * lat_rows + (part ^ other) * count
            for i in range(count):
                row = count * lons + 3 * i
                coeffs = [packet[row + k : row + k + 1, :] for k in range(3)]
                matrix = packet[i * lons : (i + 1) * lons, :]
                put(ops, weights, place(pieces, lats, first + i), flipped, matrix, coeffs)
    for lat in range(lat_rows):
        at = place(pieces, lats, me * lat_rows + lat)
        ops[at] = own_ops[lat]
        weights[at] = own_weights[lat]
    for at in range(lats):
        state[at] = given[at]
    steps(state, ops, weights, STEPS)
    fold = lons // width
    short = width // fold
    for at in range(lats):
        lat = place(pieces, lats, at)
        turned = state[at].T
        for sub in range(fold):
            index = lat * fold + sub
            out[index % pieces * cols + index // pieces] = jnp.concatenate(
                [
                    turned[sub * width + i * short : sub * width + (i + 1) * short]
                    for i in range(fold)
                ],
                axis=1,
            )


def second_kernel(pieces, cols, lat_rows, moved, ops, weights, *refs):
    lats, lons = ops.shape[0], ops.shape[2]
    count = STEPS + LAGS
    me = lax.axis_index("rows")
    outs = refs[: pieces - 1]
    if pieces == 2:
        rest, edge, state = refs[1:]
    else:
        rest, state = refs[pieces - 1 :]
    width = state.shape[1]
    fold = lons // width
    short = width // fold
    for at in range(lats):
        lat = place(pieces, lats, at)
        got = []
        for sub in range(fold):
            index = lat * fold + sub
            got.append(moved[index % pieces * cols + index // pieces])
        for i in range(fold):
            state[at, i * short : (i + 1) * short, :] = jnp.concatenate(
                [block[:, i * width : (i + 1) * width] for block in got], axis=1
            )
    if pieces == 2:
        for step in range(count):
            last = min(lats, lat_rows + count - 1 - step)
            edge[step] = advance(state, ops, weights, 0, last, None)
        for at in range(lat_rows, lats):
            rest[at - lat_rows] = state[at]
    else:
        steps(state, ops, weights, count)
        for lat in range(lat_rows):
            rest[:, lat * lons : (lat + 1) * lons] = state[me * lat_rows + lat]
    for partner in range(1, pieces):
        for lat in range(lat_rows):
            at = place(pieces, lats, (me ^ partner) * lat_rows + lat)
            outs[partner - 1][:, lat * lons : (lat + 1) * lons] = state[at]


def rest_kernel(rest, edge, ops, weights, out, state):
    lat_rows = rest.shape[0]
    lats, lons = ops.shape[0], ops.shape[2]
    count = STEPS + LAGS
    me = lax.axis_index("rows")
    for at in range(lat_rows):
        state[lat_rows + at] = rest[at]
    for step in range(count):
        first = min(lats, lat_rows + count - 1 - step)
        if first < lats:
            advance(state, ops, weights, first, lats, edge[step])
    for lat in range(lat_rows):
        out[:, lat * lons : (lat + 1) * lons] = state[place(2, lats, me * lat_rows + lat)]


def join_kernel(pieces, *refs):
    blocks, out, stack, held, sems = refs[:pieces], *refs[pieces:]
    me = lax.axis_index("rows")
    width, tall = blocks[0].shape
    chunk = min(tall, 128)
    for partner in range(pieces):
        stack[me ^ partner] = blocks[partner][...]
    copies = []
    for first in range(0, tall, chunk):
        rows = jnp.concatenate([stack[i, :, first : first + chunk] for i in range(pieces)], axis=0)
        held[first : first + chunk, :] = rows.T
        copies.append(
            pltpu.make_async_copy(
                held.at[pl.ds(first, chunk)], out.at[pl.ds(first, chunk)], sems.at[first // chunk]
            )
        )
        copies[-1].start()
    for copy in copies:
        copy.wait()


def on_device(covariance, zonal, stencil):
    pieces = lax.axis_size("rows")
    cols = lax.axis_size("cols")
    tall, wide = covariance.shape
    lat_rows, lons = zonal.shape[:2]
    lats = lat_rows * pieces
    width = wide // pieces
    share = 4
    count = lat_rows // share
    chunks = tall // min(tall, 128)

    def row_swap(value, partner):
        return lax.ppermute(value, "rows", [(i, i ^ partner) for i in range(pieces)])

    def col_swap(value, partner):
        return lax.ppermute(value, "cols", [(i, i ^ partner) for i in range(cols)])

    coeffs = stencil.transpose(1, 0, 2)
    rows = count * lons + -(-3 * count // 8) * 8
    packet = call(
        functools.partial(packet_kernel, share),
        jax.ShapeDtypeStruct((rows, lons), F32),
        (zonal, coeffs),
        [pltpu.VMEM(coeffs.shape, F32), pltpu.SemaphoreType.DMA((count + 1,))],
        [HBM, HBM],
        moved=rows * lons * 8,
    )
    strip = jax.ShapeDtypeStruct((width, tall), F32)
    cut = call(
        functools.partial(cut_kernel, pieces),
        [strip] * pieces,
        (covariance, packet),
        [pltpu.VMEM((tall, wide), F32), pltpu.SemaphoreType.DMA((chunks,))],
        [HBM, VMEM],
        moved=tall * wide * 8,
    )
    packets = []
    for partner in range(1, pieces):
        direct = row_swap(packet, partner)
        across = col_swap(direct, 2)
        packets += [direct, col_swap(direct, 1), across, col_swap(across, 1)]
    blocks = [cut[0]] + [row_swap(cut[partner], partner) for partner in range(1, pieces)]
    state = pltpu.VMEM((lats, width, lons), F32)

    def operators(number):
        return [
            jax.ShapeDtypeStruct((number, 3 * lons, lons), BF16),
            jax.ShapeDtypeStruct((number, 8, lons), F32),
        ]

    loaded = call(
        functools.partial(load_kernel, pieces),
        [jax.ShapeDtypeStruct((lats, width, lons), F32)] + operators(lat_rows),
        (*blocks, zonal, coeffs),
        flops=10**10,
        moved=10**7,
    )
    sent, ops, weights = call(
        functools.partial(first_kernel, pieces, share, cols),
        [jax.ShapeDtypeStruct((pieces * cols, width * width // lons, lons), F32)] + operators(lats),
        (*packets, *loaded),
        [state],
        flops=STEPS * lats * lons * lons * width * 6,
    )
    moved = lax.all_to_all(sent, ("rows", "cols"), 0, 0, tiled=True)
    if pieces == 2:
        end, rest, edge = call(
            functools.partial(second_kernel, pieces, cols, lat_rows),
            [
                strip,
                jax.ShapeDtypeStruct((lat_rows, width, lons), F32),
                jax.ShapeDtypeStruct((STEPS + LAGS, width, lons), F32),
            ],
            (moved, ops, weights),
            [state],
            flops=(STEPS + LAGS) * lats * lons * lons * width * 6,
        )
        ends = [end]
        mine = call(
            rest_kernel,
            strip,
            (rest, edge, ops, weights),
            [state],
            flops=(STEPS + LAGS) * lat_rows * lons * lons * width * 6,
        )
    else:
        *ends, mine = call(
            functools.partial(second_kernel, pieces, cols, lat_rows),
            [strip] * pieces,
            (moved, ops, weights),
            [state],
            flops=(STEPS + LAGS) * lats * lons * lons * width * 6,
        )
    blocks = [mine] + [row_swap(ends[partner - 1], partner) for partner in range(1, pieces)]
    return pl.pallas_call(
        functools.partial(join_kernel, pieces),
        out_shape=jax.ShapeDtypeStruct((tall, wide), F32),
        in_specs=[VMEM] * pieces,
        out_specs=HBM,
        scratch_shapes=[
            pltpu.VMEM((pieces, width, tall), F32),
            pltpu.VMEM((tall, wide), F32),
            pltpu.SemaphoreType.DMA((chunks,)),
        ],
        compiler_params=pltpu.CompilerParams(vmem_limit_bytes=LIMIT),
    )(*blocks)


def solution(mesh):
    placed = (P("rows", "cols"), P("rows", None, None), P("rows", None, None))
    return jax.shard_map(
        on_device, mesh=mesh, in_specs=placed, out_specs=P("rows", "cols"), check_vma=False
    )
```

```python
import functools

import jax
import jax.numpy as jnp
from jax import lax
from jax.experimental import pallas as pl
from jax.experimental.pallas import tpu as pltpu
from jax.sharding import PartitionSpec as P

STEPS = 3
LAGS = 3
VMEM = pl.BlockSpec(memory_space=pltpu.VMEM)
HBM = pl.BlockSpec(memory_space=pltpu.HBM)
LIMIT = 32 * 1024 * 1024
F32 = jnp.float32
FLOPS = 10**9
BF16 = jnp.bfloat16


def split(value):
    high = value.astype(BF16)
    low = (value - high.astype(F32)).astype(BF16)
    return high, low


def call(kernel, out_shape, args, scratch=(), specs=None, flops=0, moved=0):
    single = not isinstance(out_shape, (list, tuple))
    return pl.pallas_call(
        kernel,
        out_shape=out_shape,
        in_specs=specs or [VMEM] * len(args),
        out_specs=VMEM if single else [VMEM] * len(out_shape),
        scratch_shapes=list(scratch),
        compiler_params=pltpu.CompilerParams(vmem_limit_bytes=LIMIT),
        cost_estimate=pl.CostEstimate(flops=flops, bytes_accessed=moved, transcendentals=0),
    )(*args)


def place(pieces, lats, lat):
    if pieces != 2:
        return lat
    return jnp.where(lax.axis_index("rows") == 0, lats - 1 - lat, lat)


def advance(state, ops, weights, first, last, before, beyond=None, shift=0):
    lats = state.shape[0]
    own = state[first]
    for at in range(first, last):
        after = None
        if at + 1 < lats:
            after = state[at + 1] if beyond is None or at + 1 < last else beyond
        mixed = weights[at - shift, 0:1, :] * own
        if after is not None:
            mixed = mixed + weights[at - shift, 1:2, :] * after
        if before is not None:
            mixed = mixed + weights[at - shift, 2:3, :] * before
        high, low = split(mixed)
        state[at] = jnp.dot(
            jnp.concatenate([high, low, high], axis=1), ops[at - shift], preferred_element_type=F32
        )
        before, own = own, after
    return before


def packet_kernel(share, zonal, stencil, packet, stencil_out, sems):
    part = lax.axis_index("cols") % share
    lat_rows, lons = zonal.shape[:2]
    count = lat_rows // share
    copies = [pltpu.make_async_copy(stencil, stencil_out, sems.at[count])]
    for i in range(count):
        target = packet.at[pl.ds(i * lons, lons)]
        copies.append(pltpu.make_async_copy(zonal.at[part * count + i], target, sems.at[i]))
    for copy in copies:
        copy.start()
    copies[0].wait()
    for i in range(count):
        for k in range(3):
            row = count * lons + 3 * i + k
            packet[row : row + 1, :] = stencil_out[k, pl.ds(part * count + i, 1), :]
    for copy in copies[1:]:
        copy.wait()


def merge_kernel(*refs):
    *packets, out = refs
    for i, packet in enumerate(packets):
        out[i] = packet[...]


def put(ops, weights, at, flipped, matrix, coeffs):
    high, low = split(matrix.T)
    ops[at] = jnp.concatenate([high, high, low], axis=0)
    own, north, south = coeffs
    weights[at, 0:1, :] = own
    weights[at, 1:2, :] = jnp.where(flipped, south, north)
    weights[at, 2:3, :] = jnp.where(flipped, north, south)


def steps(state, ops, weights, count):
    lats = state.shape[0]

    def one(step, carry):
        advance(state, ops, weights, 0, lats, None)
        return carry

    lax.fori_loop(0, count, one, 0, unroll=lats * count <= 128)


def cut_kernel(pieces, block, zonal, stencil, *refs):
    outs, ops, weights = refs[:pieces], *refs[pieces : pieces + 2]
    held, matrices, sems = refs[pieces + 2 :]
    me = lax.axis_index("rows")
    tall, wide = block.shape
    lat_rows = zonal.shape[0]
    lats = pieces * lat_rows
    width = wide // pieces
    chunk = min(tall, 128)
    starts = range(0, tall, chunk)
    copies = [
        pltpu.make_async_copy(
            block.at[pl.ds(first, chunk)], held.at[pl.ds(first, chunk)], sems.at[first // chunk]
        )
        for first in starts
    ]
    copies += [
        pltpu.make_async_copy(zonal.at[lat], matrices.at[lat], sems.at[len(starts) + lat])
        for lat in range(lat_rows)
    ]
    for copy in copies:
        copy.start()
    for copy in copies[: len(starts)]:
        copy.wait()
    for first in starts:
        turned = held[first : first + chunk, :].T
        for partner in range(pieces):
            piece = turned[:width]
            for other in range(1, pieces):
                piece = jnp.where((me ^ partner) == other, turned[other * width : (other + 1) * width], piece)
            outs[partner][:, first : first + chunk] = piece
    for copy in copies[len(starts) :]:
        copy.wait()
    flipped = place(pieces, lats, 0) != 0
    for lat in range(lat_rows):
        coeffs = [stencil[k, lat : lat + 1, :] for k in range(3)]
        at = place(2, lats, me * lat_rows + lat) - lat_rows if pieces == 2 else lat
        put(ops, weights, at, flipped, matrices[lat], coeffs)


def load_kernel(pieces, lat_rows, *refs):
    blocks = refs[:pieces]
    if pieces == 2:
        own_ops, own_weights, state, edge = refs[pieces:]
    else:
        state = refs[pieces]
    me = lax.axis_index("rows")
    lats, lons = state.shape[0], state.shape[2]
    for partner in range(pieces):
        for lat in range(lat_rows):
            at = place(pieces, lats, (me ^ partner) * lat_rows + lat)
            state[at] = blocks[partner][:, lat * lons : (lat + 1) * lons]
    if pieces == 2:
        for step in range(STEPS):
            first = lat_rows + step
            edge[step] = state[first]
            advance(state, own_ops, own_weights, first, lats, state[first - 1], shift=lat_rows)


def first_kernel(pieces, cols, hops, *refs):
    n_packets = 2 * (pieces - 1)
    packets = refs[:n_packets]
    own_ops, own_weights, given = refs[n_packets : n_packets + 3]
    out, ops, weights, state = refs[-4:]
    share = 2 * len(hops)
    me = lax.axis_index("rows")
    part = lax.axis_index("cols") % share
    lats, width, lons = state.shape
    lat_rows = lats // pieces
    count = lat_rows // share
    flipped = place(pieces, lats, 0) != 0
    for lat in range(lat_rows):
        at = lat_rows + lat if pieces == 2 else me * lat_rows + lat
        ops[at] = own_ops[lat]
        weights[at] = own_weights[lat]
    for partner in range(1, pieces):
        for core in range(2):
            packet = packets[2 * (partner - 1) + core]
            for at, hop in enumerate(hops):
                for i in range(count):
                    lat = (me ^ partner) * lat_rows + (part ^ hop ^ core) * count + i
                    row = count * lons + 3 * i
                    coeffs = [packet[at, row + k : row + k + 1, :] for k in range(3)]
                    matrix = packet[at, i * lons : (i + 1) * lons, :]
                    put(ops, weights, place(pieces, lats, lat), flipped, matrix, coeffs)
    for at in range(lats):
        state[at] = given[at]
    if pieces == 2:
        edge = refs[n_packets + 3]
        for step in range(STEPS):
            advance(state, ops, weights, 0, lat_rows + step, None, edge[step])
    else:
        steps(state, ops, weights, STEPS)
    fold = lons // width
    short = width // fold
    for at in range(lats):
        lat = place(pieces, lats, at)
        turned = state[at].T
        for sub in range(fold):
            index = lat * fold + sub
            out[index % pieces * cols + index // pieces] = jnp.concatenate(
                [
                    turned[sub * width + i * short : sub * width + (i + 1) * short]
                    for i in range(fold)
                ],
                axis=1,
            )


def second_kernel(pieces, cols, lat_rows, moved, ops, weights, *refs):
    lats, lons = ops.shape[0], ops.shape[2]
    count = STEPS + LAGS
    me = lax.axis_index("rows")
    outs = refs[: pieces - 1]
    if pieces == 2:
        rest, edge, state = refs[1:]
    else:
        rest, state = refs[pieces - 1 :]
    width = state.shape[1]
    fold = lons // width
    short = width // fold
    for at in range(lats):
        lat = place(pieces, lats, at)
        got = []
        for sub in range(fold):
            index = lat * fold + sub
            got.append(moved[index % pieces * cols + index // pieces])
        for i in range(fold):
            state[at, i * short : (i + 1) * short, :] = jnp.concatenate(
                [block[:, i * width : (i + 1) * width] for block in got], axis=1
            )
    if pieces == 2:
        for step in range(count):
            last = min(lats, lat_rows + count - 1 - step)
            edge[step] = advance(state, ops, weights, 0, last, None)
        for at in range(lat_rows, lats):
            rest[at - lat_rows] = state[at]
    else:
        steps(state, ops, weights, count)
        for lat in range(lat_rows):
            rest[:, lat * lons : (lat + 1) * lons] = state[me * lat_rows + lat]
    for partner in range(1, pieces):
        for lat in range(lat_rows):
            at = place(pieces, lats, (me ^ partner) * lat_rows + lat)
            outs[partner - 1][:, lat * lons : (lat + 1) * lons] = state[at]


def rest_kernel(rest, edge, ops, weights, out, state):
    lat_rows = rest.shape[0]
    lats, lons = ops.shape[0], ops.shape[2]
    count = STEPS + LAGS
    me = lax.axis_index("rows")
    for at in range(lat_rows):
        state[lat_rows + at] = rest[at]
    for step in range(count):
        first = min(lats, lat_rows + count - 1 - step)
        if first < lats:
            advance(state, ops, weights, first, lats, edge[step])
    for lat in range(lat_rows):
        out[:, lat * lons : (lat + 1) * lons] = state[place(2, lats, me * lat_rows + lat)]


def join_kernel(pieces, *refs):
    blocks, out, stack, held, sems = refs[:pieces], *refs[pieces:]
    me = lax.axis_index("rows")
    width, tall = blocks[0].shape
    chunk = min(tall, 128)
    for partner in range(pieces):
        stack[me ^ partner] = blocks[partner][...]
    copies = []
    for first in range(0, tall, chunk):
        rows = jnp.concatenate([stack[i, :, first : first + chunk] for i in range(pieces)], axis=0)
        held[first : first + chunk, :] = rows.T
        copies.append(
            pltpu.make_async_copy(
                held.at[pl.ds(first, chunk)], out.at[pl.ds(first, chunk)], sems.at[first // chunk]
            )
        )
        copies[-1].start()
    for copy in copies:
        copy.wait()


def on_device(covariance, zonal, stencil):
    pieces = lax.axis_size("rows")
    cols = lax.axis_size("cols")
    tall, wide = covariance.shape
    lat_rows, lons = zonal.shape[:2]
    lats = lat_rows * pieces
    width = wide // pieces
    hops = (0, 2, 4, 6) if lat_rows % 8 == 0 and cols % 8 == 0 else (0,)
    share = 2 * len(hops)
    count = lat_rows // share
    chunks = tall // min(tall, 128)

    def row_swap(value, partner):
        return lax.ppermute(value, "rows", [(i, i ^ partner) for i in range(pieces)])

    def col_swap(value, partner):
        return lax.ppermute(value, "cols", [(i, i ^ partner) for i in range(cols)])

    coeffs = pltpu.with_memory_space_constraint(stencil.transpose(1, 0, 2), pltpu.HBM)
    given = pltpu.with_memory_space_constraint(zonal, pltpu.HBM)
    block = pltpu.with_memory_space_constraint(covariance, pltpu.HBM)
    rows = count * lons + -(-3 * count // 8) * 8
    strip = jax.ShapeDtypeStruct((width, tall), F32)

    def operators(number):
        return [
            jax.ShapeDtypeStruct((number, 3 * lons, lons), BF16),
            jax.ShapeDtypeStruct((number, 8, lons), F32),
        ]

    packet, held_coeffs = call(
        functools.partial(packet_kernel, share),
        [jax.ShapeDtypeStruct((rows, lons), F32), jax.ShapeDtypeStruct(coeffs.shape, F32)],
        (given, coeffs),
        [pltpu.SemaphoreType.DMA((count + 1,))],
        [HBM, HBM],
        moved=10**5,
    )
    *cut, own_ops, own_weights = call(
        functools.partial(cut_kernel, pieces),
        [strip] * pieces + operators(lat_rows),
        (block, given, held_coeffs),
        [
            pltpu.VMEM((tall, wide), F32),
            pltpu.VMEM(zonal.shape, F32),
            pltpu.SemaphoreType.DMA((chunks + lat_rows,)),
        ],
        [HBM, HBM, VMEM],
        moved=tall * wide * 8,
    )
    packets = []
    blocks = [cut[0]]
    for partner in range(1, pieces):
        direct = row_swap(packet, partner)
        merged = call(
            merge_kernel,
            jax.ShapeDtypeStruct((len(hops), rows, lons), F32),
            [direct] + [col_swap(direct, hop) for hop in hops[1:]],
            moved=10**5,
        )
        packets += [merged, col_swap(merged, 1)]
        blocks.append(row_swap(cut[partner], partner))
    states = [jax.ShapeDtypeStruct((lats, width, lons), F32)]
    own = [own_ops, own_weights]
    if pieces == 2:
        states.append(jax.ShapeDtypeStruct((STEPS, width, lons), F32))
    loaded = call(
        functools.partial(load_kernel, pieces, lat_rows),
        states,
        blocks + own if pieces == 2 else blocks,
        flops=FLOPS,
        moved=10**6,
    )
    state = pltpu.VMEM((lats, width, lons), F32)
    sent, ops, weights = call(
        functools.partial(first_kernel, pieces, cols, hops),
        [jax.ShapeDtypeStruct((pieces * cols, width * width // lons, lons), F32)] + operators(lats),
        (*packets, *own, *loaded),
        [state],
        flops=STEPS * lats * lons * lons * width * 6,
    )
    moved = lax.all_to_all(sent, ("rows", "cols"), 0, 0, tiled=True)
    if pieces == 2:
        end, rest, edge = call(
            functools.partial(second_kernel, pieces, cols, lat_rows),
            [
                strip,
                jax.ShapeDtypeStruct((lat_rows, width, lons), F32),
                jax.ShapeDtypeStruct((STEPS + LAGS, width, lons), F32),
            ],
            (moved, ops, weights),
            [state],
            flops=(STEPS + LAGS) * lats * lons * lons * width * 6,
        )
        ends = [end]
        mine = call(
            rest_kernel,
            strip,
            (rest, edge, ops, weights),
            [state],
            flops=(STEPS + LAGS) * lat_rows * lons * lons * width * 6,
        )
    else:
        *ends, mine = call(
            functools.partial(second_kernel, pieces, cols, lat_rows),
            [strip] * pieces,
            (moved, ops, weights),
            [state],
            flops=(STEPS + LAGS) * lats * lons * lons * width * 6,
        )
    blocks = [mine] + [row_swap(ends[partner - 1], partner) for partner in range(1, pieces)]
    return pl.pallas_call(
        functools.partial(join_kernel, pieces),
        out_shape=jax.ShapeDtypeStruct((tall, wide), F32),
        in_specs=[VMEM] * pieces,
        out_specs=HBM,
        scratch_shapes=[
            pltpu.VMEM((pieces, width, tall), F32),
            pltpu.VMEM((tall, wide), F32),
            pltpu.SemaphoreType.DMA((chunks,)),
        ],
        compiler_params=pltpu.CompilerParams(vmem_limit_bytes=LIMIT),
    )(*blocks)


def solution(mesh):
    placed = (P("rows", "cols"), P("rows", None, None), P("rows", None, None))
    return jax.shard_map(
        on_device, mesh=mesh, in_specs=placed, out_specs=P("rows", "cols"), check_vma=False
    )
```

```python
import functools

import jax
import jax.numpy as jnp
from jax import lax
from jax.experimental import pallas as pl
from jax.experimental.pallas import tpu as pltpu
from jax.sharding import PartitionSpec as P

STEPS = 3
LAGS = 3
VMEM = pl.BlockSpec(memory_space=pltpu.VMEM)
HBM = pl.BlockSpec(memory_space=pltpu.HBM)
LIMIT = 32 * 1024 * 1024
F32 = jnp.float32
FLOPS = 10**9
BF16 = jnp.bfloat16


def split(value):
    high = value.astype(BF16)
    low = (value - high.astype(F32)).astype(BF16)
    return high, low


def call(kernel, out_shape, args, scratch=(), specs=None, flops=0, moved=0):
    single = not isinstance(out_shape, (list, tuple))
    return pl.pallas_call(
        kernel,
        out_shape=out_shape,
        in_specs=specs or [VMEM] * len(args),
        out_specs=VMEM if single else [VMEM] * len(out_shape),
        scratch_shapes=list(scratch),
        compiler_params=pltpu.CompilerParams(vmem_limit_bytes=LIMIT),
        cost_estimate=pl.CostEstimate(flops=flops, bytes_accessed=moved, transcendentals=0),
    )(*args)


def place(pieces, lats, lat):
    if pieces != 2:
        return lat
    return jnp.where(lax.axis_index("rows") == 0, lats - 1 - lat, lat)


def advance(state, ops, weights, first, last, before, beyond=None, shift=0):
    lats = state.shape[0]
    own = state[first]
    for at in range(first, last):
        after = None
        if at + 1 < lats:
            after = state[at + 1] if beyond is None or at + 1 < last else beyond
        mixed = weights[at - shift, 0:1, :] * own
        if after is not None:
            mixed = mixed + weights[at - shift, 1:2, :] * after
        if before is not None:
            mixed = mixed + weights[at - shift, 2:3, :] * before
        high, low = split(mixed)
        state[at] = jnp.dot(
            jnp.concatenate([high, low, high], axis=1), ops[at - shift], preferred_element_type=F32
        )
        before, own = own, after
    return before


def packet_kernel(share, zonal, stencil, packet, stencil_out, sems):
    part = lax.axis_index("cols") % share
    lat_rows, lons = zonal.shape[:2]
    count = lat_rows // share
    copies = [pltpu.make_async_copy(stencil, stencil_out, sems.at[count])]
    for i in range(count):
        target = packet.at[pl.ds(i * lons, lons)]
        copies.append(pltpu.make_async_copy(zonal.at[part * count + i], target, sems.at[i]))
    for copy in copies:
        copy.start()
    copies[0].wait()
    for i in range(count):
        for k in range(3):
            row = count * lons + 3 * i + k
            packet[row : row + 1, :] = stencil_out[k, pl.ds(part * count + i, 1), :]
    for copy in copies[1:]:
        copy.wait()


def merge_kernel(*refs):
    *packets, out = refs
    for i, packet in enumerate(packets):
        out[i] = packet[...]


def put(ops, weights, at, flipped, matrix, coeffs):
    high, low = split(matrix.T)
    ops[at] = jnp.concatenate([high, high, low], axis=0)
    own, north, south = coeffs
    weights[at, 0:1, :] = own
    weights[at, 1:2, :] = jnp.where(flipped, south, north)
    weights[at, 2:3, :] = jnp.where(flipped, north, south)


def steps(state, ops, weights, count):
    lats = state.shape[0]

    def one(step, carry):
        advance(state, ops, weights, 0, lats, None)
        return carry

    lax.fori_loop(0, count, one, 0, unroll=lats * count <= 128)


def cut_kernel(pieces, block, zonal, stencil, *refs):
    outs, ops, weights = refs[:pieces], *refs[pieces : pieces + 2]
    held, matrices, sems = refs[pieces + 2 :]
    me = lax.axis_index("rows")
    tall, wide = block.shape
    lat_rows = zonal.shape[0]
    lats = pieces * lat_rows
    width = wide // pieces
    chunk = min(tall, 128)
    starts = range(0, tall, chunk)
    copies = [
        pltpu.make_async_copy(
            block.at[pl.ds(first, chunk)], held.at[pl.ds(first, chunk)], sems.at[first // chunk]
        )
        for first in starts
    ]
    copies += [
        pltpu.make_async_copy(zonal.at[lat], matrices.at[lat], sems.at[len(starts) + lat])
        for lat in range(lat_rows)
    ]
    for copy in copies:
        copy.start()
    for copy in copies[: len(starts)]:
        copy.wait()
    for first in starts:
        turned = held[first : first + chunk, :].T
        for partner in range(pieces):
            piece = turned[:width]
            for other in range(1, pieces):
                piece = jnp.where((me ^ partner) == other, turned[other * width : (other + 1) * width], piece)
            outs[partner][:, first : first + chunk] = piece
    for copy in copies[len(starts) :]:
        copy.wait()
    flipped = place(pieces, lats, 0) != 0
    for lat in range(lat_rows):
        coeffs = [stencil[k, lat : lat + 1, :] for k in range(3)]
        at = place(2, lats, me * lat_rows + lat) - lat_rows if pieces == 2 else lat
        put(ops, weights, at, flipped, matrices[lat], coeffs)


def load_kernel(pieces, lat_rows, *refs):
    blocks = refs[:pieces]
    if pieces == 2:
        own_ops, own_weights, state, edge = refs[pieces:]
    else:
        state = refs[pieces]
    me = lax.axis_index("rows")
    lats, lons = state.shape[0], state.shape[2]
    for partner in range(pieces):
        for lat in range(lat_rows):
            at = place(pieces, lats, (me ^ partner) * lat_rows + lat)
            state[at] = blocks[partner][:, lat * lons : (lat + 1) * lons]
    if pieces == 2:
        for step in range(STEPS):
            first = lat_rows + step
            edge[step] = state[first]
            advance(state, own_ops, own_weights, first, lats, state[first - 1], shift=lat_rows)


def first_kernel(pieces, cols, hops, *refs):
    n_packets = 2 * (pieces - 1)
    packets = refs[:n_packets]
    own_ops, own_weights, given = refs[n_packets : n_packets + 3]
    out, ops, weights, state = refs[-4:]
    share = 2 * len(hops)
    me = lax.axis_index("rows")
    part = lax.axis_index("cols") % share
    lats, width, lons = state.shape
    lat_rows = lats // pieces
    count = lat_rows // share
    flipped = place(pieces, lats, 0) != 0
    for lat in range(lat_rows):
        at = lat_rows + lat if pieces == 2 else me * lat_rows + lat
        ops[at] = own_ops[lat]
        weights[at] = own_weights[lat]
    for partner in range(1, pieces):
        for core in range(2):
            packet = packets[2 * (partner - 1) + core]
            for at, hop in enumerate(hops):
                for i in range(count):
                    lat = (me ^ partner) * lat_rows + (part ^ hop ^ core) * count + i
                    row = count * lons + 3 * i
                    coeffs = [packet[at, row + k : row + k + 1, :] for k in range(3)]
                    matrix = packet[at, i * lons : (i + 1) * lons, :]
                    put(ops, weights, place(pieces, lats, lat), flipped, matrix, coeffs)
    for at in range(lats):
        state[at] = given[at]
    if pieces == 2:
        edge = refs[n_packets + 3]
        for step in range(STEPS):
            advance(state, ops, weights, 0, lat_rows + step, None, edge[step])
    else:
        steps(state, ops, weights, STEPS)
    fold = lons // width
    short = width // fold
    for at in range(lats):
        lat = place(pieces, lats, at)
        turned = state[at].T
        for sub in range(fold):
            index = lat * fold + sub
            out[index % pieces * cols + index // pieces] = jnp.concatenate(
                [
                    turned[sub * width + i * short : sub * width + (i + 1) * short]
                    for i in range(fold)
                ],
                axis=1,
            )


def unpack(pieces, cols, moved, state):
    lats, width, lons = state.shape
    fold = lons // width
    short = width // fold
    for at in range(lats):
        lat = place(pieces, lats, at)
        got = []
        for sub in range(fold):
            index = lat * fold + sub
            got.append(moved[index % pieces * cols + index // pieces])
        for i in range(fold):
            state[at, i * short : (i + 1) * short, :] = jnp.concatenate(
                [block[:, i * width : (i + 1) * width] for block in got], axis=1
            )


def second_kernel(pieces, cols, lat_rows, moved, ops, weights, *refs):
    *outs, state = refs
    lons = ops.shape[2]
    me = lax.axis_index("rows")
    unpack(pieces, cols, moved, state)
    steps(state, ops, weights, STEPS + LAGS)
    for partner in range(pieces):
        for lat in range(lat_rows):
            outs[partner][:, lat * lons : (lat + 1) * lons] = state[(me ^ partner) * lat_rows + lat]


def stage_kernel(cols, low, high, groups, *refs):
    count = STEPS + LAGS
    state = refs[-1]
    lats, width, lons = state.shape
    if low == 0:
        moved, ops, weights = refs[:3]
        outs = refs[3:-1]
        unpack(2, cols, moved, state)
    else:
        rest, edge, ops, weights = refs[:4]
        outs = refs[4:-1]
        for at in range(low, lats):
            state[at] = rest[at - low]
    for step in range(count):
        further = count - 1 - step
        first = low + further if low else 0
        last = min(lats, high + further) if high < lats else lats
        if first < last:
            before = advance(state, ops, weights, first, last, edge[step] if low else None)
            if high < lats:
                outs[-1][step] = before
    if high < lats:
        for at in range(high, lats):
            outs[-2][at - high] = state[at]
    flipped = place(2, lats, 0) != 0
    for out, (start, stop) in zip(outs, groups):
        for i in range(stop - start):
            out[:, i * lons : (i + 1) * lons] = state[jnp.where(flipped, stop - 1 - i, start + i)]


def join_kernel(pieces, lons, start, stop, *refs):
    stack, held, sems = refs[-3:]
    blocks, out = refs[:pieces], refs[-4]
    me = lax.axis_index("rows")
    base = 0
    if pieces == 2:
        lat_rows = out.shape[0] // lons
        base = pl.multiple_of(jnp.where(me == 0, start, lat_rows - stop) * lons, lons)
    for partner in range(pieces):
        stack[me ^ partner] = blocks[partner][...]
    copies = []
    for at in range(stop - start):
        first = at * lons
        rows = jnp.concatenate([stack[i, :, first : first + lons] for i in range(pieces)], axis=0)
        held[first : first + lons, :] = rows.T
        copies.append(
            pltpu.make_async_copy(
                held.at[pl.ds(first, lons)], out.at[pl.ds(base + first, lons)], sems.at[at]
            )
        )
        copies[-1].start()
    for copy in copies:
        copy.wait()


def join(pieces, lons, start, stop, shape, blocks, given=None):
    width = blocks[0].shape[0]
    size = stop - start
    return pl.pallas_call(
        functools.partial(join_kernel, pieces, lons, start, stop),
        out_shape=jax.ShapeDtypeStruct(shape, F32),
        in_specs=[VMEM] * pieces + ([] if given is None else [HBM]),
        out_specs=HBM,
        scratch_shapes=[
            pltpu.VMEM((pieces, width, size * lons), F32),
            pltpu.VMEM((size * lons, shape[1]), F32),
            pltpu.SemaphoreType.DMA((size,)),
        ],
        input_output_aliases={} if given is None else {pieces: 0},
        compiler_params=pltpu.CompilerParams(vmem_limit_bytes=LIMIT),
    )(*blocks, *([] if given is None else [given]))


def on_device(covariance, zonal, stencil):
    pieces = lax.axis_size("rows")
    cols = lax.axis_size("cols")
    tall, wide = covariance.shape
    lat_rows, lons = zonal.shape[:2]
    lats = lat_rows * pieces
    width = wide // pieces
    hops = (0, 2, 4, 6) if lat_rows % 8 == 0 and cols % 8 == 0 else (0,)
    share = 2 * len(hops)
    count = lat_rows // share
    chunks = tall // min(tall, 128)

    def row_swap(value, partner):
        return lax.ppermute(value, "rows", [(i, i ^ partner) for i in range(pieces)])

    def col_swap(value, partner):
        return lax.ppermute(value, "cols", [(i, i ^ partner) for i in range(cols)])

    coeffs = pltpu.with_memory_space_constraint(stencil.transpose(1, 0, 2), pltpu.HBM)
    given = pltpu.with_memory_space_constraint(zonal, pltpu.HBM)
    block = pltpu.with_memory_space_constraint(covariance, pltpu.HBM)
    rows = count * lons + -(-3 * count // 8) * 8
    strip = jax.ShapeDtypeStruct((width, tall), F32)

    def operators(number):
        return [
            jax.ShapeDtypeStruct((number, 3 * lons, lons), BF16),
            jax.ShapeDtypeStruct((number, 8, lons), F32),
        ]

    packet, held_coeffs = call(
        functools.partial(packet_kernel, share),
        [jax.ShapeDtypeStruct((rows, lons), F32), jax.ShapeDtypeStruct(coeffs.shape, F32)],
        (given, coeffs),
        [pltpu.SemaphoreType.DMA((count + 1,))],
        [HBM, HBM],
        moved=10**5,
    )
    *cut, own_ops, own_weights = call(
        functools.partial(cut_kernel, pieces),
        [strip] * pieces + operators(lat_rows),
        (block, given, held_coeffs),
        [
            pltpu.VMEM((tall, wide), F32),
            pltpu.VMEM(zonal.shape, F32),
            pltpu.SemaphoreType.DMA((chunks + lat_rows,)),
        ],
        [HBM, HBM, VMEM],
        moved=tall * wide * 8,
    )
    packets = []
    blocks = [cut[0]]
    for partner in range(1, pieces):
        direct = row_swap(packet, partner)
        merged = call(
            merge_kernel,
            jax.ShapeDtypeStruct((len(hops), rows, lons), F32),
            [direct] + [col_swap(direct, hop) for hop in hops[1:]],
            moved=10**5,
        )
        packets += [merged, col_swap(merged, 1)]
        blocks.append(row_swap(cut[partner], partner))
    states = [jax.ShapeDtypeStruct((lats, width, lons), F32)]
    own = [own_ops, own_weights]
    if pieces == 2:
        states.append(jax.ShapeDtypeStruct((STEPS, width, lons), F32))
    loaded = call(
        functools.partial(load_kernel, pieces, lat_rows),
        states,
        blocks + own if pieces == 2 else blocks,
        flops=FLOPS,
        moved=10**6,
    )
    state = pltpu.VMEM((lats, width, lons), F32)
    sent, ops, weights = call(
        functools.partial(first_kernel, pieces, cols, hops),
        [jax.ShapeDtypeStruct((pieces * cols, width * width // lons, lons), F32)] + operators(lats),
        (*packets, *own, *loaded),
        [state],
        flops=STEPS * lats * lons * lons * width * 6,
    )
    moved = lax.all_to_all(sent, ("rows", "cols"), 0, 0, tiled=True)
    if pieces != 2:
        mine, *ends = call(
            functools.partial(second_kernel, pieces, cols, lat_rows),
            [strip] * pieces,
            (moved, ops, weights),
            [state],
            flops=(STEPS + LAGS) * lats * lons * lons * width * 6,
        )
        blocks = [mine] + [row_swap(ends[partner - 1], partner) for partner in range(1, pieces)]
        return join(pieces, lons, 0, lat_rows, (tall, wide), blocks)

    def group(start, stop):
        return jax.ShapeDtypeStruct((width, (stop - start) * lons), F32)

    cuts = [0, lat_rows // 2, lat_rows] if lat_rows % 2 == 0 else [0, lat_rows]
    given = (moved,)
    got = []
    for low, high in zip(cuts, cuts[1:]):
        end, rest, edge = call(
            functools.partial(stage_kernel, cols, low, high, ((low, high),)),
            [
                group(low, high),
                jax.ShapeDtypeStruct((lats - high, width, lons), F32),
                jax.ShapeDtypeStruct((STEPS + LAGS, width, lons), F32),
            ],
            (*given, ops, weights),
            [state],
            flops=10**7,
        )
        got.append(row_swap(end, 1))
        given = (rest, edge)
    mirror = [(lats - high, lats - low) for low, high in zip(cuts, cuts[1:])]
    mine = call(
        functools.partial(stage_kernel, cols, lat_rows, lats, mirror),
        [group(*span) for span in mirror],
        (*given, ops, weights),
        [state],
        flops=10**7,
    )
    out = None
    for low, high, own, other in zip(cuts, cuts[1:], mine, got):
        out = join(2, lons, low, high, (tall, wide), [own, other], out)
    return out


def solution(mesh):
    placed = (P("rows", "cols"), P("rows", None, None), P("rows", None, None))
    return jax.shard_map(
        on_device, mesh=mesh, in_specs=placed, out_specs=P("rows", "cols"), check_vma=False
    )
```

```python
import functools

import jax
import jax.numpy as jnp
from jax import lax
from jax.experimental import pallas as pl
from jax.experimental.pallas import tpu as pltpu
from jax.sharding import PartitionSpec as P

STEPS = 3
LAGS = 3
VMEM = pl.BlockSpec(memory_space=pltpu.VMEM)
HBM = pl.BlockSpec(memory_space=pltpu.HBM)
LIMIT = 32 * 1024 * 1024
F32 = jnp.float32
FLOPS = 5 * 10**8
LATE = 10**9
BF16 = jnp.bfloat16


def split(value):
    high = value.astype(BF16)
    low = (value - high.astype(F32)).astype(BF16)
    return high, low


def call(kernel, out_shape, args, scratch=(), specs=None, flops=0, moved=0):
    single = not isinstance(out_shape, (list, tuple))
    return pl.pallas_call(
        kernel,
        out_shape=out_shape,
        in_specs=specs or [VMEM] * len(args),
        out_specs=VMEM if single else [VMEM] * len(out_shape),
        scratch_shapes=list(scratch),
        compiler_params=pltpu.CompilerParams(vmem_limit_bytes=LIMIT),
        cost_estimate=pl.CostEstimate(flops=flops, bytes_accessed=moved, transcendentals=0),
    )(*args)


def place(pieces, lats, lat):
    if pieces != 2:
        return lat
    return jnp.where(lax.axis_index("rows") == 0, lats - 1 - lat, lat)


def advance(state, ops, weights, first, last, before, beyond=None, shift=0):
    lats = state.shape[0]
    own = state[first]
    for at in range(first, last):
        after = None
        if at + 1 < lats:
            after = state[at + 1] if beyond is None or at + 1 < last else beyond
        mixed = weights[at - shift, 0:1, :] * own
        if after is not None:
            mixed = mixed + weights[at - shift, 1:2, :] * after
        if before is not None:
            mixed = mixed + weights[at - shift, 2:3, :] * before
        high, low = split(mixed)
        state[at] = jnp.dot(
            jnp.concatenate([high, low, high], axis=1), ops[at - shift], preferred_element_type=F32
        )
        before, own = own, after
    return before


def packet_kernel(share, zonal, stencil, packet, stencil_out, sems):
    part = lax.axis_index("cols") % share
    lat_rows, lons = zonal.shape[:2]
    count = lat_rows // share
    copies = [pltpu.make_async_copy(stencil, stencil_out, sems.at[count])]
    for i in range(count):
        target = packet.at[pl.ds(i * lons, lons)]
        copies.append(pltpu.make_async_copy(zonal.at[part * count + i], target, sems.at[i]))
    for copy in copies:
        copy.start()
    copies[0].wait()
    for i in range(count):
        for k in range(3):
            row = count * lons + 3 * i + k
            packet[row : row + 1, :] = stencil_out[k, pl.ds(part * count + i, 1), :]
    for copy in copies[1:]:
        copy.wait()


def merge_kernel(count, *refs):
    *packets, out = refs
    lons = out.shape[2]
    for at, packet in enumerate(packets):
        for i in range(count):
            out[at, i * lons : (i + 1) * lons, :] = packet[i * lons : (i + 1) * lons, :].T
        out[at, count * lons :, :] = packet[count * lons :, :]


def put(ops, weights, at, flipped, turned, coeffs):
    high, low = split(turned)
    ops[at] = jnp.concatenate([high, high, low], axis=0)
    own, north, south = coeffs
    weights[at, 0:1, :] = own
    weights[at, 1:2, :] = jnp.where(flipped, south, north)
    weights[at, 2:3, :] = jnp.where(flipped, north, south)


def steps(state, ops, weights, count):
    lats = state.shape[0]

    def one(step, carry):
        advance(state, ops, weights, 0, lats, None)
        return carry

    lax.fori_loop(0, count, one, 0, unroll=lats * count <= 128)


def cut_kernel(pieces, block, zonal, stencil, *refs):
    outs, ops, weights = refs[:pieces], *refs[pieces : pieces + 2]
    held, matrices, sems = refs[pieces + 2 :]
    me = lax.axis_index("rows")
    tall, wide = block.shape
    lat_rows = zonal.shape[0]
    lats = pieces * lat_rows
    width = wide // pieces
    chunk = min(tall, 128)
    starts = range(0, tall, chunk)
    copies = [
        pltpu.make_async_copy(
            block.at[pl.ds(first, chunk)], held.at[pl.ds(first, chunk)], sems.at[first // chunk]
        )
        for first in starts
    ]
    copies += [
        pltpu.make_async_copy(zonal.at[lat], matrices.at[lat], sems.at[len(starts) + lat])
        for lat in range(lat_rows)
    ]
    for copy in copies:
        copy.start()
    for copy in copies[: len(starts)]:
        copy.wait()
    for first in starts:
        turned = held[first : first + chunk, :].T
        for partner in range(pieces):
            piece = turned[:width]
            for other in range(1, pieces):
                piece = jnp.where((me ^ partner) == other, turned[other * width : (other + 1) * width], piece)
            outs[partner][:, first : first + chunk] = piece
    for copy in copies[len(starts) :]:
        copy.wait()
    flipped = place(pieces, lats, 0) != 0
    for lat in range(lat_rows):
        coeffs = [stencil[k, lat : lat + 1, :] for k in range(3)]
        at = place(2, lats, me * lat_rows + lat) - lat_rows if pieces == 2 else lat
        put(ops, weights, at, flipped, matrices[lat].T, coeffs)


def load_kernel(pieces, lat_rows, *refs):
    blocks = refs[:pieces]
    if pieces == 2:
        own_ops, own_weights, state, edge = refs[pieces:]
    else:
        state = refs[pieces]
    me = lax.axis_index("rows")
    lats, lons = state.shape[0], state.shape[2]
    for partner in range(pieces):
        for lat in range(lat_rows):
            at = place(pieces, lats, (me ^ partner) * lat_rows + lat)
            state[at] = blocks[partner][:, lat * lons : (lat + 1) * lons]
    if pieces == 2:
        for step in range(STEPS):
            first = lat_rows + step
            edge[step] = state[first]
            advance(state, own_ops, own_weights, first, lats, state[first - 1], shift=lat_rows)


def first_kernel(pieces, cols, hops, *refs):
    n_packets = (2 if len(hops) == 1 else 4) * (pieces - 1)
    packets = refs[:n_packets]
    own_ops, own_weights, given = refs[n_packets : n_packets + 3]
    out, ops, weights, state = refs[-4:]
    share = 2 * len(hops)
    me = lax.axis_index("rows")
    part = lax.axis_index("cols") % share
    lats, width, lons = state.shape
    lat_rows = lats // pieces
    count = lat_rows // share
    flipped = place(pieces, lats, 0) != 0
    for lat in range(lat_rows):
        at = lat_rows + lat if pieces == 2 else me * lat_rows + lat
        ops[at] = own_ops[lat]
        weights[at] = own_weights[lat]
    early = hops[:1] + hops[2:]
    late = hops[1:2]
    for partner in range(1, pieces):
        for group, of_group in enumerate([early, late] if late else [early]):
            for core in range(2):
                packet = packets[(n_packets // (pieces - 1)) * (partner - 1) + 2 * group + core]
                for at, hop in enumerate(of_group):
                    for i in range(count):
                        lat = (me ^ partner) * lat_rows + (part ^ hop ^ core) * count + i
                        row = count * lons + 3 * i
                        coeffs = [packet[at, row + k : row + k + 1, :] for k in range(3)]
                        turned = packet[at, i * lons : (i + 1) * lons, :]
                        put(ops, weights, place(pieces, lats, lat), flipped, turned, coeffs)
    for at in range(lats):
        state[at] = given[at]
    if pieces == 2:
        edge = refs[n_packets + 3]
        for step in range(STEPS):
            advance(state, ops, weights, 0, lat_rows + step, None, edge[step])
    else:
        steps(state, ops, weights, STEPS)
    fold = lons // width
    short = width // fold
    for at in range(lats):
        lat = place(pieces, lats, at)
        turned = state[at].T
        for sub in range(fold):
            index = lat * fold + sub
            out[index % pieces * cols + index // pieces] = jnp.concatenate(
                [
                    turned[sub * width + i * short : sub * width + (i + 1) * short]
                    for i in range(fold)
                ],
                axis=1,
            )


def unpack(pieces, cols, moved, state):
    lats, width, lons = state.shape
    fold = lons // width
    short = width // fold
    for at in range(lats):
        lat = place(pieces, lats, at)
        got = []
        for sub in range(fold):
            index = lat * fold + sub
            got.append(moved[index % pieces * cols + index // pieces])
        for i in range(fold):
            state[at, i * short : (i + 1) * short, :] = jnp.concatenate(
                [block[:, i * width : (i + 1) * width] for block in got], axis=1
            )


def second_kernel(pieces, cols, lat_rows, moved, ops, weights, *refs):
    *outs, state = refs
    lons = ops.shape[2]
    me = lax.axis_index("rows")
    unpack(pieces, cols, moved, state)
    steps(state, ops, weights, STEPS + LAGS)
    for partner in range(pieces):
        for lat in range(lat_rows):
            outs[partner][:, lat * lons : (lat + 1) * lons] = state[(me ^ partner) * lat_rows + lat]


def stage_kernel(cols, low, high, groups, *refs):
    count = STEPS + LAGS
    state = refs[-1]
    lats, width, lons = state.shape
    if low == 0:
        moved, ops, weights = refs[:3]
        outs = refs[3:-1]
        unpack(2, cols, moved, state)
    else:
        rest, edge, ops, weights = refs[:4]
        outs = refs[4:-1]
        for at in range(low, lats):
            state[at] = rest[at - low]
    for step in range(count):
        further = count - 1 - step
        first = low + further if low else 0
        last = min(lats, high + further) if high < lats else lats
        if first < last:
            before = advance(state, ops, weights, first, last, edge[step] if low else None)
            if high < lats:
                outs[-1][step] = before
    if high < lats:
        for at in range(high, lats):
            outs[-2][at - high] = state[at]
    flipped = place(2, lats, 0) != 0
    for out, (start, stop) in zip(outs, groups):
        for i in range(stop - start):
            out[:, i * lons : (i + 1) * lons] = state[jnp.where(flipped, stop - 1 - i, start + i)]


def join_kernel(pieces, lons, start, stop, *refs):
    stack, held, sems = refs[-3:]
    blocks, out = refs[:pieces], refs[-4]
    me = lax.axis_index("rows")
    base = 0
    if pieces == 2:
        lat_rows = out.shape[0] // lons
        base = pl.multiple_of(jnp.where(me == 0, start, lat_rows - stop) * lons, lons)
    for partner in range(pieces):
        stack[me ^ partner] = blocks[partner][...]
    copies = []
    for at in range(stop - start):
        first = at * lons
        rows = jnp.concatenate([stack[i, :, first : first + lons] for i in range(pieces)], axis=0)
        held[first : first + lons, :] = rows.T
        copies.append(
            pltpu.make_async_copy(
                held.at[pl.ds(first, lons)], out.at[pl.ds(base + first, lons)], sems.at[at]
            )
        )
        copies[-1].start()
    for copy in copies:
        copy.wait()


def join(pieces, lons, start, stop, shape, blocks, given=None):
    width = blocks[0].shape[0]
    size = stop - start
    return pl.pallas_call(
        functools.partial(join_kernel, pieces, lons, start, stop),
        out_shape=jax.ShapeDtypeStruct(shape, F32),
        in_specs=[VMEM] * pieces + ([] if given is None else [HBM]),
        out_specs=HBM,
        scratch_shapes=[
            pltpu.VMEM((pieces, width, size * lons), F32),
            pltpu.VMEM((size * lons, shape[1]), F32),
            pltpu.SemaphoreType.DMA((size,)),
        ],
        input_output_aliases={} if given is None else {pieces: 0},
        compiler_params=pltpu.CompilerParams(vmem_limit_bytes=LIMIT),
    )(*blocks, *([] if given is None else [given]))


def on_device(covariance, zonal, stencil):
    pieces = lax.axis_size("rows")
    cols = lax.axis_size("cols")
    tall, wide = covariance.shape
    lat_rows, lons = zonal.shape[:2]
    lats = lat_rows * pieces
    width = wide // pieces
    hops = (0, 2, 4, 6) if lat_rows % 8 == 0 and cols % 8 == 0 else (0,)
    share = 2 * len(hops)
    count = lat_rows // share
    chunks = tall // min(tall, 128)

    def row_swap(value, partner):
        return lax.ppermute(value, "rows", [(i, i ^ partner) for i in range(pieces)])

    def col_swap(value, partner):
        return lax.ppermute(value, "cols", [(i, i ^ partner) for i in range(cols)])

    coeffs = pltpu.with_memory_space_constraint(stencil.transpose(1, 0, 2), pltpu.HBM)
    given = pltpu.with_memory_space_constraint(zonal, pltpu.HBM)
    block = pltpu.with_memory_space_constraint(covariance, pltpu.HBM)
    rows = count * lons + -(-3 * count // 8) * 8
    strip = jax.ShapeDtypeStruct((width, tall), F32)

    def operators(number):
        return [
            jax.ShapeDtypeStruct((number, 3 * lons, lons), BF16),
            jax.ShapeDtypeStruct((number, 8, lons), F32),
        ]

    packet, held_coeffs = call(
        functools.partial(packet_kernel, share),
        [jax.ShapeDtypeStruct((rows, lons), F32), jax.ShapeDtypeStruct(coeffs.shape, F32)],
        (given, coeffs),
        [pltpu.SemaphoreType.DMA((count + 1,))],
        [HBM, HBM],
        moved=10**5,
    )
    *cut, own_ops, own_weights = call(
        functools.partial(cut_kernel, pieces),
        [strip] * pieces + operators(lat_rows),
        (block, given, held_coeffs),
        [
            pltpu.VMEM((tall, wide), F32),
            pltpu.VMEM(zonal.shape, F32),
            pltpu.SemaphoreType.DMA((chunks + lat_rows,)),
        ],
        [HBM, HBM, VMEM],
        moved=tall * wide * 8,
    )
    packets = []
    blocks = [cut[0]]
    for partner in range(1, pieces):
        direct = row_swap(packet, partner)
        across = [col_swap(direct, hop) for hop in hops[1:]]
        for group, flops in (([direct] + across[1:], 0), (across[:1], LATE)):
            if group:
                merged = call(
                    functools.partial(merge_kernel, count),
                    jax.ShapeDtypeStruct((len(group), rows, lons), F32),
                    group,
                    flops=flops,
                    moved=10**5,
                )
                packets += [merged, col_swap(merged, 1)]
        blocks.append(row_swap(cut[partner], partner))
    states = [jax.ShapeDtypeStruct((lats, width, lons), F32)]
    own = [own_ops, own_weights]
    if pieces == 2:
        states.append(jax.ShapeDtypeStruct((STEPS, width, lons), F32))
    loaded = call(
        functools.partial(load_kernel, pieces, lat_rows),
        states,
        blocks + own if pieces == 2 else blocks,
        flops=FLOPS,
        moved=10**6,
    )
    state = pltpu.VMEM((lats, width, lons), F32)
    sent, ops, weights = call(
        functools.partial(first_kernel, pieces, cols, hops),
        [jax.ShapeDtypeStruct((pieces * cols, width * width // lons, lons), F32)] + operators(lats),
        (*packets, *own, *loaded),
        [state],
        flops=STEPS * lats * lons * lons * width * 6,
    )
    moved = lax.all_to_all(sent, ("rows", "cols"), 0, 0, tiled=True)
    if pieces != 2:
        mine, *ends = call(
            functools.partial(second_kernel, pieces, cols, lat_rows),
            [strip] * pieces,
            (moved, ops, weights),
            [state],
            flops=(STEPS + LAGS) * lats * lons * lons * width * 6,
        )
        blocks = [mine] + [row_swap(ends[partner - 1], partner) for partner in range(1, pieces)]
        return join(pieces, lons, 0, lat_rows, (tall, wide), blocks)

    def group(start, stop):
        return jax.ShapeDtypeStruct((width, (stop - start) * lons), F32)

    cuts = [0, lat_rows // 2, lat_rows] if lat_rows % 2 == 0 else [0, lat_rows]
    given = (moved,)
    got = []
    for low, high in zip(cuts, cuts[1:]):
        end, rest, edge = call(
            functools.partial(stage_kernel, cols, low, high, ((low, high),)),
            [
                group(low, high),
                jax.ShapeDtypeStruct((lats - high, width, lons), F32),
                jax.ShapeDtypeStruct((STEPS + LAGS, width, lons), F32),
            ],
            (*given, ops, weights),
            [state],
            flops=10**7,
        )
        got.append(row_swap(end, 1))
        given = (rest, edge)
    mirror = [(lats - high, lats - low) for low, high in zip(cuts, cuts[1:])]
    mine = call(
        functools.partial(stage_kernel, cols, lat_rows, lats, mirror),
        [group(*span) for span in mirror],
        (*given, ops, weights),
        [state],
        flops=10**7,
    )
    out = None
    for low, high, own, other in zip(cuts, cuts[1:], mine, got):
        out = join(2, lons, low, high, (tall, wide), [own, other], out)
    return out


def solution(mesh):
    placed = (P("rows", "cols"), P("rows", None, None), P("rows", None, None))
    return jax.shard_map(
        on_device, mesh=mesh, in_specs=placed, out_specs=P("rows", "cols"), check_vma=False
    )
```

```python
import functools

import jax
import jax.numpy as jnp
from jax import lax
from jax.experimental import pallas as pl
from jax.experimental.pallas import tpu as pltpu
from jax.sharding import PartitionSpec as P

STEPS = 3
LAGS = 3
VMEM = pl.BlockSpec(memory_space=pltpu.VMEM)
HBM = pl.BlockSpec(memory_space=pltpu.HBM)
LIMIT = 32 * 1024 * 1024
F32 = jnp.float32
FLOPS = 5 * 10**8
LATE = 10**9
BF16 = jnp.bfloat16


def split(value):
    high = value.astype(BF16)
    low = (value - high.astype(F32)).astype(BF16)
    return high, low


def call(kernel, out_shape, args, scratch=(), specs=None, flops=0, moved=0):
    single = not isinstance(out_shape, (list, tuple))
    return pl.pallas_call(
        kernel,
        out_shape=out_shape,
        in_specs=specs or [VMEM] * len(args),
        out_specs=VMEM if single else [VMEM] * len(out_shape),
        scratch_shapes=list(scratch),
        compiler_params=pltpu.CompilerParams(vmem_limit_bytes=LIMIT),
        cost_estimate=pl.CostEstimate(flops=flops, bytes_accessed=moved, transcendentals=0),
    )(*args)


def place(pieces, lats, lat):
    if pieces != 2:
        return lat
    return jnp.where(lax.axis_index("rows") == 0, lats - 1 - lat, lat)


def advance(state, ops, weights, first, last, before, beyond=None, shift=0):
    lats = state.shape[0]
    own = state[first]
    for at in range(first, last):
        after = None
        if at + 1 < lats:
            after = state[at + 1] if beyond is None or at + 1 < last else beyond
        mixed = weights[at - shift, 0:1, :] * own
        if after is not None:
            mixed = mixed + weights[at - shift, 1:2, :] * after
        if before is not None:
            mixed = mixed + weights[at - shift, 2:3, :] * before
        high, low = split(mixed)
        state[at] = jnp.dot(
            jnp.concatenate([high, low, high], axis=1), ops[at - shift], preferred_element_type=F32
        )
        before, own = own, after
    return before


def packet_kernel(share, zonal, stencil, packet, stencil_out, sems):
    part = lax.axis_index("cols") % share
    lat_rows, lons = zonal.shape[:2]
    count = lat_rows // share
    copies = [pltpu.make_async_copy(stencil, stencil_out, sems.at[count])]
    for i in range(count):
        target = packet.at[pl.ds(i * lons, lons)]
        copies.append(pltpu.make_async_copy(zonal.at[part * count + i], target, sems.at[i]))
    for copy in copies:
        copy.start()
    copies[0].wait()
    for i in range(count):
        for k in range(3):
            row = count * lons + 3 * i + k
            packet[row : row + 1, :] = stencil_out[k, pl.ds(part * count + i, 1), :]
    for copy in copies[1:]:
        copy.wait()


def merge_kernel(count, *refs):
    *packets, out = refs
    lons = out.shape[2]
    for at, packet in enumerate(packets):
        for i in range(count):
            out[at, i * lons : (i + 1) * lons, :] = packet[i * lons : (i + 1) * lons, :].T
        out[at, count * lons :, :] = packet[count * lons :, :]


def put(ops, weights, at, flipped, turned, coeffs):
    high, low = split(turned)
    ops[at] = jnp.concatenate([high, high, low], axis=0)
    own, north, south = coeffs
    weights[at, 0:1, :] = own
    weights[at, 1:2, :] = jnp.where(flipped, south, north)
    weights[at, 2:3, :] = jnp.where(flipped, north, south)


def steps(state, ops, weights, count):
    lats = state.shape[0]

    def one(step, carry):
        advance(state, ops, weights, 0, lats, None)
        return carry

    lax.fori_loop(0, count, one, 0, unroll=lats * count <= 128)


def cut_kernel(pieces, block, zonal, stencil, *refs):
    outs, ops, weights = refs[:pieces], *refs[pieces : pieces + 2]
    held, matrices, sems = refs[pieces + 2 :]
    me = lax.axis_index("rows")
    tall, wide = block.shape
    lat_rows = zonal.shape[0]
    lats = pieces * lat_rows
    width = wide // pieces
    chunk = min(tall, 128)
    starts = range(0, tall, chunk)
    copies = [
        pltpu.make_async_copy(
            block.at[pl.ds(first, chunk)], held.at[pl.ds(first, chunk)], sems.at[first // chunk]
        )
        for first in starts
    ]
    copies += [
        pltpu.make_async_copy(zonal.at[lat], matrices.at[lat], sems.at[len(starts) + lat])
        for lat in range(lat_rows)
    ]
    for copy in copies:
        copy.start()
    for copy in copies[: len(starts)]:
        copy.wait()
    for first in starts:
        turned = held[first : first + chunk, :].T
        for partner in range(pieces):
            piece = turned[:width]
            for other in range(1, pieces):
                piece = jnp.where((me ^ partner) == other, turned[other * width : (other + 1) * width], piece)
            outs[partner][:, first : first + chunk] = piece
    for copy in copies[len(starts) :]:
        copy.wait()
    flipped = place(pieces, lats, 0) != 0
    for lat in range(lat_rows):
        coeffs = [stencil[k, lat : lat + 1, :] for k in range(3)]
        at = place(2, lats, me * lat_rows + lat) - lat_rows if pieces == 2 else lat
        put(ops, weights, at, flipped, matrices[lat].T, coeffs)


def load_kernel(pieces, lat_rows, *refs):
    blocks = refs[:pieces]
    if pieces == 2:
        own_ops, own_weights, state, edge = refs[pieces:]
    else:
        state = refs[pieces]
    me = lax.axis_index("rows")
    lats, lons = state.shape[0], state.shape[2]
    for partner in range(pieces):
        for lat in range(lat_rows):
            at = place(pieces, lats, (me ^ partner) * lat_rows + lat)
            state[at] = blocks[partner][:, lat * lons : (lat + 1) * lons]
    if pieces == 2:
        for step in range(STEPS):
            first = lat_rows + step
            edge[step] = state[first]
            advance(state, own_ops, own_weights, first, lats, state[first - 1], shift=lat_rows)


def first_kernel(pieces, cols, hops, *refs):
    n_packets = (2 if len(hops) == 1 else 4) * (pieces - 1)
    packets = refs[:n_packets]
    own_ops, own_weights, given = refs[n_packets : n_packets + 3]
    out, ops, weights, state = refs[-4:]
    share = 2 * len(hops)
    me = lax.axis_index("rows")
    part = lax.axis_index("cols") % share
    lats, width, lons = state.shape
    lat_rows = lats // pieces
    count = lat_rows // share
    flipped = place(pieces, lats, 0) != 0
    for lat in range(lat_rows):
        at = lat_rows + lat if pieces == 2 else me * lat_rows + lat
        ops[at] = own_ops[lat]
        weights[at] = own_weights[lat]
    early = hops[:1] + hops[2:]
    late = hops[1:2]
    for partner in range(1, pieces):
        for group, of_group in enumerate([early, late] if late else [early]):
            for core in range(2):
                packet = packets[(n_packets // (pieces - 1)) * (partner - 1) + 2 * group + core]
                for at, hop in enumerate(of_group):
                    for i in range(count):
                        lat = (me ^ partner) * lat_rows + (part ^ hop ^ core) * count + i
                        row = count * lons + 3 * i
                        coeffs = [packet[at, row + k : row + k + 1, :] for k in range(3)]
                        turned = packet[at, i * lons : (i + 1) * lons, :]
                        put(ops, weights, place(pieces, lats, lat), flipped, turned, coeffs)
    for at in range(lats):
        state[at] = given[at]
    if pieces == 2:
        edge = refs[n_packets + 3]
        for step in range(STEPS):
            advance(state, ops, weights, 0, lat_rows + step, None, edge[step])
    else:
        steps(state, ops, weights, STEPS)
    fold = lons // width
    short = width // fold
    for at in range(lats):
        lat = place(pieces, lats, at)
        turned = state[at].T
        for sub in range(fold):
            index = lat * fold + sub
            out[index % pieces * cols + index // pieces] = jnp.concatenate(
                [
                    turned[sub * width + i * short : sub * width + (i + 1) * short]
                    for i in range(fold)
                ],
                axis=1,
            )


def unpack(pieces, cols, moved, state):
    lats, width, lons = state.shape
    fold = lons // width
    short = width // fold
    for at in range(lats):
        lat = place(pieces, lats, at)
        got = []
        for sub in range(fold):
            index = lat * fold + sub
            got.append(moved[index % pieces * cols + index // pieces])
        for i in range(fold):
            state[at, i * short : (i + 1) * short, :] = jnp.concatenate(
                [block[:, i * width : (i + 1) * width] for block in got], axis=1
            )


def second_kernel(pieces, cols, lat_rows, moved, ops, weights, *refs):
    *outs, state = refs
    lons = ops.shape[2]
    me = lax.axis_index("rows")
    unpack(pieces, cols, moved, state)
    steps(state, ops, weights, STEPS + LAGS)
    for partner in range(pieces):
        for lat in range(lat_rows):
            outs[partner][:, lat * lons : (lat + 1) * lons] = state[(me ^ partner) * lat_rows + lat]


def stage_kernel(cols, low, high, groups, *refs):
    count = STEPS + LAGS
    state = refs[-1]
    lats, width, lons = state.shape
    if low == 0:
        moved, ops, weights = refs[:3]
        outs = refs[3:-1]
        unpack(2, cols, moved, state)
    else:
        rest, edge, ops, weights = refs[:4]
        outs = refs[4:-1]
        for at in range(low, lats):
            state[at] = rest[at - low]
    for step in range(count):
        further = count - 1 - step
        first = low + further if low else 0
        last = min(lats, high + further) if high < lats else lats
        if first < last:
            before = advance(state, ops, weights, first, last, edge[step] if low else None)
            if high < lats:
                outs[-1][step] = before
    if high < lats:
        for at in range(high, lats):
            outs[-2][at - high] = state[at]
    flipped = place(2, lats, 0) != 0
    for out, (start, stop) in zip(outs, groups):
        for i in range(stop - start):
            out[:, i * lons : (i + 1) * lons] = state[jnp.where(flipped, stop - 1 - i, start + i)]


def join_kernel(pieces, lons, start, stop, *refs):
    stack, held, sems = refs[-3:]
    blocks, out = refs[:pieces], refs[-4]
    me = lax.axis_index("rows")
    base = 0
    if pieces == 2:
        lat_rows = out.shape[0] // lons
        base = pl.multiple_of(jnp.where(me == 0, start, lat_rows - stop) * lons, lons)
    for partner in range(pieces):
        stack[me ^ partner] = blocks[partner][...]
    copies = []
    for at in range(stop - start):
        first = at * lons
        rows = jnp.concatenate([stack[i, :, first : first + lons] for i in range(pieces)], axis=0)
        held[first : first + lons, :] = rows.T
        copies.append(
            pltpu.make_async_copy(
                held.at[pl.ds(first, lons)], out.at[pl.ds(base + first, lons)], sems.at[at]
            )
        )
        copies[-1].start()
    for copy in copies:
        copy.wait()


def join(pieces, lons, start, stop, shape, blocks, given=None):
    width = blocks[0].shape[0]
    size = stop - start
    return pl.pallas_call(
        functools.partial(join_kernel, pieces, lons, start, stop),
        out_shape=jax.ShapeDtypeStruct(shape, F32),
        in_specs=[VMEM] * pieces + ([] if given is None else [HBM]),
        out_specs=HBM,
        scratch_shapes=[
            pltpu.VMEM((pieces, width, size * lons), F32),
            pltpu.VMEM((size * lons, shape[1]), F32),
            pltpu.SemaphoreType.DMA((size,)),
        ],
        input_output_aliases={} if given is None else {pieces: 0},
        compiler_params=pltpu.CompilerParams(vmem_limit_bytes=LIMIT),
    )(*blocks, *([] if given is None else [given]))


def on_device(covariance, zonal, stencil):
    pieces = lax.axis_size("rows")
    cols = lax.axis_size("cols")
    tall, wide = covariance.shape
    lat_rows, lons = zonal.shape[:2]
    lats = lat_rows * pieces
    width = wide // pieces
    hops = (0, 6, 2, 4) if lat_rows % 8 == 0 and cols % 8 == 0 else (0,)
    share = 2 * len(hops)
    count = lat_rows // share
    chunks = tall // min(tall, 128)

    def row_swap(value, partner):
        return lax.ppermute(value, "rows", [(i, i ^ partner) for i in range(pieces)])

    def col_swap(value, partner):
        return lax.ppermute(value, "cols", [(i, i ^ partner) for i in range(cols)])

    coeffs = pltpu.with_memory_space_constraint(stencil.transpose(1, 0, 2), pltpu.HBM)
    given = pltpu.with_memory_space_constraint(zonal, pltpu.HBM)
    block = pltpu.with_memory_space_constraint(covariance, pltpu.HBM)
    rows = count * lons + -(-3 * count // 8) * 8
    strip = jax.ShapeDtypeStruct((width, tall), F32)

    def operators(number):
        return [
            jax.ShapeDtypeStruct((number, 3 * lons, lons), BF16),
            jax.ShapeDtypeStruct((number, 8, lons), F32),
        ]

    packet, held_coeffs = call(
        functools.partial(packet_kernel, share),
        [jax.ShapeDtypeStruct((rows, lons), F32), jax.ShapeDtypeStruct(coeffs.shape, F32)],
        (given, coeffs),
        [pltpu.SemaphoreType.DMA((count + 1,))],
        [HBM, HBM],
        moved=10**5,
    )
    *cut, own_ops, own_weights = call(
        functools.partial(cut_kernel, pieces),
        [strip] * pieces + operators(lat_rows),
        (block, given, held_coeffs),
        [
            pltpu.VMEM((tall, wide), F32),
            pltpu.VMEM(zonal.shape, F32),
            pltpu.SemaphoreType.DMA((chunks + lat_rows,)),
        ],
        [HBM, HBM, VMEM],
        moved=tall * wide * 8,
    )
    packets = []
    blocks = [cut[0]]
    for partner in range(1, pieces):
        direct = row_swap(packet, partner)
        across = [col_swap(direct, hop) for hop in hops[1:]]
        for group, flops in (([direct] + across[1:], 0), (across[:1], LATE)):
            if group:
                merged = call(
                    functools.partial(merge_kernel, count),
                    jax.ShapeDtypeStruct((len(group), rows, lons), F32),
                    group,
                    flops=flops,
                    moved=10**5,
                )
                packets += [merged, col_swap(merged, 1)]
        blocks.append(row_swap(cut[partner], partner))
    states = [jax.ShapeDtypeStruct((lats, width, lons), F32)]
    own = [own_ops, own_weights]
    if pieces == 2:
        states.append(jax.ShapeDtypeStruct((STEPS, width, lons), F32))
    loaded = call(
        functools.partial(load_kernel, pieces, lat_rows),
        states,
        blocks + own if pieces == 2 else blocks,
        flops=FLOPS,
        moved=10**6,
    )
    state = pltpu.VMEM((lats, width, lons), F32)
    sent, ops, weights = call(
        functools.partial(first_kernel, pieces, cols, hops),
        [jax.ShapeDtypeStruct((pieces * cols, width * width // lons, lons), F32)] + operators(lats),
        (*packets, *own, *loaded),
        [state],
        flops=STEPS * lats * lons * lons * width * 6,
    )
    moved = lax.all_to_all(sent, ("rows", "cols"), 0, 0, tiled=True)
    if pieces != 2:
        mine, *ends = call(
            functools.partial(second_kernel, pieces, cols, lat_rows),
            [strip] * pieces,
            (moved, ops, weights),
            [state],
            flops=(STEPS + LAGS) * lats * lons * lons * width * 6,
        )
        blocks = [mine] + [row_swap(ends[partner - 1], partner) for partner in range(1, pieces)]
        return join(pieces, lons, 0, lat_rows, (tall, wide), blocks)

    def group(start, stop):
        return jax.ShapeDtypeStruct((width, (stop - start) * lons), F32)

    cuts = [0, lat_rows // 2, lat_rows] if lat_rows % 2 == 0 else [0, lat_rows]
    given = (moved,)
    got = []
    for low, high in zip(cuts, cuts[1:]):
        end, rest, edge = call(
            functools.partial(stage_kernel, cols, low, high, ((low, high),)),
            [
                group(low, high),
                jax.ShapeDtypeStruct((lats - high, width, lons), F32),
                jax.ShapeDtypeStruct((STEPS + LAGS, width, lons), F32),
            ],
            (*given, ops, weights),
            [state],
            flops=10**7,
        )
        got.append(row_swap(end, 1))
        given = (rest, edge)
    mirror = [(lats - high, lats - low) for low, high in zip(cuts, cuts[1:])]
    mine = call(
        functools.partial(stage_kernel, cols, lat_rows, lats, mirror),
        [group(*span) for span in mirror],
        (*given, ops, weights),
        [state],
        flops=10**7,
    )
    out = None
    for low, high, own, other in zip(cuts, cuts[1:], mine, got):
        out = join(2, lons, low, high, (tall, wide), [own, other], out)
    return out


def solution(mesh):
    placed = (P("rows", "cols"), P("rows", None, None), P("rows", None, None))
    return jax.shard_map(
        on_device, mesh=mesh, in_specs=placed, out_specs=P("rows", "cols"), check_vma=False
    )
```

```python
import functools

import jax
import jax.numpy as jnp
from jax import lax
from jax.experimental import pallas as pl
from jax.experimental.pallas import tpu as pltpu
from jax.sharding import PartitionSpec as P

STEPS = 3
LAGS = 3
VMEM = pl.BlockSpec(memory_space=pltpu.VMEM)
HBM = pl.BlockSpec(memory_space=pltpu.HBM)
LIMIT = 32 * 1024 * 1024
F32 = jnp.float32
FLOPS = 5 * 10**8
LATE = 10**9
BF16 = jnp.bfloat16


def split(value):
    high = value.astype(BF16)
    low = (value - high.astype(F32)).astype(BF16)
    return high, low


def call(kernel, out_shape, args, scratch=(), specs=None, flops=0, moved=0):
    single = not isinstance(out_shape, (list, tuple))
    return pl.pallas_call(
        kernel,
        out_shape=out_shape,
        in_specs=specs or [VMEM] * len(args),
        out_specs=VMEM if single else [VMEM] * len(out_shape),
        scratch_shapes=list(scratch),
        compiler_params=pltpu.CompilerParams(vmem_limit_bytes=LIMIT),
        cost_estimate=pl.CostEstimate(flops=flops, bytes_accessed=moved, transcendentals=0),
    )(*args)


def place(pieces, lats, lat):
    if pieces != 2:
        return lat
    return jnp.where(lax.axis_index("rows") == 0, lats - 1 - lat, lat)


def advance(state, ops, weights, first, last, before, beyond=None, shift=0):
    lats = state.shape[0]
    own = state[first]
    for at in range(first, last):
        after = None
        if at + 1 < lats:
            after = state[at + 1] if beyond is None or at + 1 < last else beyond
        mixed = weights[at - shift, 0:1, :] * own
        if after is not None:
            mixed = mixed + weights[at - shift, 1:2, :] * after
        if before is not None:
            mixed = mixed + weights[at - shift, 2:3, :] * before
        high, low = split(mixed)
        state[at] = jnp.dot(
            jnp.concatenate([high, low, high], axis=1), ops[at - shift], preferred_element_type=F32
        )
        before, own = own, after
    return before


def packet_kernel(share, zonal, stencil, packet, stencil_out, sems):
    part = lax.axis_index("cols") % share
    lat_rows, lons = zonal.shape[:2]
    count = lat_rows // share
    copies = [pltpu.make_async_copy(stencil, stencil_out, sems.at[count])]
    for i in range(count):
        target = packet.at[pl.ds(i * lons, lons)]
        copies.append(pltpu.make_async_copy(zonal.at[part * count + i], target, sems.at[i]))
    for copy in copies:
        copy.start()
    copies[0].wait()
    for i in range(count):
        for k in range(3):
            row = count * lons + 3 * i + k
            packet[row : row + 1, :] = stencil_out[k, pl.ds(part * count + i, 1), :]
    for copy in copies[1:]:
        copy.wait()


def merge_kernel(count, *refs):
    *packets, out = refs
    lons = out.shape[2]
    for at, packet in enumerate(packets):
        for i in range(count):
            out[at, i * lons : (i + 1) * lons, :] = packet[i * lons : (i + 1) * lons, :].T
        out[at, count * lons :, :] = packet[count * lons :, :]


def put(ops, weights, at, flipped, turned, coeffs):
    high, low = split(turned)
    ops[at] = jnp.concatenate([high, high, low], axis=0)
    own, north, south = coeffs
    weights[at, 0:1, :] = own
    weights[at, 1:2, :] = jnp.where(flipped, south, north)
    weights[at, 2:3, :] = jnp.where(flipped, north, south)


def steps(state, ops, weights, count):
    lats = state.shape[0]

    def one(step, carry):
        advance(state, ops, weights, 0, lats, None)
        return carry

    lax.fori_loop(0, count, one, 0, unroll=lats * count <= 128)


def cut_kernel(pieces, block, zonal, stencil, *refs):
    outs, ops, weights = refs[:pieces], *refs[pieces : pieces + 2]
    held, matrices, sems = refs[pieces + 2 :]
    me = lax.axis_index("rows")
    tall, wide = block.shape
    lat_rows = zonal.shape[0]
    lats = pieces * lat_rows
    width = wide // pieces
    chunk = min(tall, 128)
    starts = range(0, tall, chunk)
    copies = [
        pltpu.make_async_copy(
            block.at[pl.ds(first, chunk)], held.at[pl.ds(first, chunk)], sems.at[first // chunk]
        )
        for first in starts
    ]
    copies += [
        pltpu.make_async_copy(zonal.at[lat], matrices.at[lat], sems.at[len(starts) + lat])
        for lat in range(lat_rows)
    ]
    for copy in copies:
        copy.start()
    for copy in copies[: len(starts)]:
        copy.wait()
    for first in starts:
        turned = held[first : first + chunk, :].T
        for partner in range(pieces):
            piece = turned[:width]
            for other in range(1, pieces):
                piece = jnp.where((me ^ partner) == other, turned[other * width : (other + 1) * width], piece)
            outs[partner][:, first : first + chunk] = piece
    for copy in copies[len(starts) :]:
        copy.wait()
    flipped = place(pieces, lats, 0) != 0
    for lat in range(lat_rows):
        coeffs = [stencil[k, lat : lat + 1, :] for k in range(3)]
        at = place(2, lats, me * lat_rows + lat) - lat_rows if pieces == 2 else lat
        put(ops, weights, at, flipped, matrices[lat].T, coeffs)


def load_kernel(pieces, lat_rows, *refs):
    blocks = refs[:pieces]
    if pieces == 2:
        own_ops, own_weights, state, edge = refs[pieces:]
    else:
        state = refs[pieces]
    me = lax.axis_index("rows")
    lats, lons = state.shape[0], state.shape[2]
    for partner in range(pieces):
        for lat in range(lat_rows):
            at = place(pieces, lats, (me ^ partner) * lat_rows + lat)
            state[at] = blocks[partner][:, lat * lons : (lat + 1) * lons]
    if pieces == 2:
        for step in range(STEPS):
            first = lat_rows + step
            edge[step] = state[first]
            advance(state, own_ops, own_weights, first, lats, state[first - 1], shift=lat_rows)


def first_kernel(pieces, cols, hops, *refs):
    n_packets = (2 if len(hops) == 1 else 4) * (pieces - 1)
    packets = refs[:n_packets]
    own_ops, own_weights, given = refs[n_packets : n_packets + 3]
    out, ops, weights, state = refs[-4:]
    share = 2 * len(hops)
    me = lax.axis_index("rows")
    part = lax.axis_index("cols") % share
    lats, width, lons = state.shape
    lat_rows = lats // pieces
    count = lat_rows // share
    flipped = place(pieces, lats, 0) != 0
    for lat in range(lat_rows):
        at = lat_rows + lat if pieces == 2 else me * lat_rows + lat
        ops[at] = own_ops[lat]
        weights[at] = own_weights[lat]
    early = hops[:1] + hops[2:]
    late = hops[1:2]
    for partner in range(1, pieces):
        for group, of_group in enumerate([early, late] if late else [early]):
            for core in range(2):
                packet = packets[(n_packets // (pieces - 1)) * (partner - 1) + 2 * group + core]
                for at, hop in enumerate(of_group):
                    for i in range(count):
                        lat = (me ^ partner) * lat_rows + (part ^ hop ^ core) * count + i
                        row = count * lons + 3 * i
                        coeffs = [packet[at, row + k : row + k + 1, :] for k in range(3)]
                        turned = packet[at, i * lons : (i + 1) * lons, :]
                        put(ops, weights, place(pieces, lats, lat), flipped, turned, coeffs)
    for at in range(lats):
        state[at] = given[at]
    if pieces == 2:
        edge = refs[n_packets + 3]
        for step in range(STEPS):
            advance(state, ops, weights, 0, lat_rows + step, None, edge[step])
    else:
        steps(state, ops, weights, STEPS)
    fold = lons // width
    short = width // fold
    for at in range(lats):
        lat = place(pieces, lats, at)
        turned = state[at].T
        for sub in range(fold):
            index = lat * fold + sub
            out[index % pieces * cols + index // pieces] = jnp.concatenate(
                [
                    turned[sub * width + i * short : sub * width + (i + 1) * short]
                    for i in range(fold)
                ],
                axis=1,
            )


def unpack(pieces, cols, moved, state):
    lats, width, lons = state.shape
    fold = lons // width
    short = width // fold
    for at in range(lats):
        lat = place(pieces, lats, at)
        got = []
        for sub in range(fold):
            index = lat * fold + sub
            got.append(moved[index % pieces * cols + index // pieces])
        for i in range(fold):
            state[at, i * short : (i + 1) * short, :] = jnp.concatenate(
                [block[:, i * width : (i + 1) * width] for block in got], axis=1
            )


def second_kernel(pieces, cols, lat_rows, moved, ops, weights, *refs):
    *outs, state = refs
    lons = ops.shape[2]
    me = lax.axis_index("rows")
    unpack(pieces, cols, moved, state)
    steps(state, ops, weights, STEPS + LAGS)
    for partner in range(pieces):
        for lat in range(lat_rows):
            outs[partner][:, lat * lons : (lat + 1) * lons] = state[(me ^ partner) * lat_rows + lat]


def stage_kernel(cols, low, high, groups, *refs):
    count = STEPS + LAGS
    state = refs[-1]
    lats, width, lons = state.shape
    if low == 0:
        moved, ops, weights = refs[:3]
        outs = refs[3:-1]
        unpack(2, cols, moved, state)
    else:
        rest, edge, ops, weights = refs[:4]
        outs = refs[4:-1]
        for at in range(low, lats):
            state[at] = rest[at - low]
    for step in range(count):
        further = count - 1 - step
        first = low + further if low else 0
        last = min(lats, high + further) if high < lats else lats
        if first < last:
            before = advance(state, ops, weights, first, last, edge[step] if low else None)
            if high < lats:
                outs[-1][step] = before
    if high < lats:
        for at in range(high, lats):
            outs[-2][at - high] = state[at]
    flipped = place(2, lats, 0) != 0
    for out, (start, stop) in zip(outs, groups):
        for i in range(stop - start):
            out[:, i * lons : (i + 1) * lons] = state[jnp.where(flipped, stop - 1 - i, start + i)]


def join_kernel(pieces, lons, start, stop, *refs):
    held, sems = refs[-2:]
    blocks, out = refs[:pieces], refs[-3]
    me = lax.axis_index("rows")
    base = 0
    if pieces == 2:
        lat_rows = out.shape[0] // lons
        base = pl.multiple_of(jnp.where(me == 0, start, lat_rows - stop) * lons, lons)
    copies = []
    for at in range(stop - start):
        first = at * lons
        found = [block[:, first : first + lons] for block in blocks]
        parts = []
        for i in range(pieces):
            part = found[0]
            for partner in range(1, pieces):
                part = jnp.where((me ^ partner) == i, found[partner], part)
            parts.append(part)
        rows = jnp.concatenate(parts, axis=0)
        held[first : first + lons, :] = rows.T
        copies.append(
            pltpu.make_async_copy(
                held.at[pl.ds(first, lons)], out.at[pl.ds(base + first, lons)], sems.at[at]
            )
        )
        copies[-1].start()
    for copy in copies:
        copy.wait()


def join(pieces, lons, start, stop, shape, blocks, given=None):
    size = stop - start
    return pl.pallas_call(
        functools.partial(join_kernel, pieces, lons, start, stop),
        out_shape=jax.ShapeDtypeStruct(shape, F32),
        in_specs=[VMEM] * pieces + ([] if given is None else [HBM]),
        out_specs=HBM,
        scratch_shapes=[
            pltpu.VMEM((size * lons, shape[1]), F32),
            pltpu.SemaphoreType.DMA((size,)),
        ],
        input_output_aliases={} if given is None else {pieces: 0},
        compiler_params=pltpu.CompilerParams(vmem_limit_bytes=LIMIT),
    )(*blocks, *([] if given is None else [given]))


def on_device(covariance, zonal, stencil):
    pieces = lax.axis_size("rows")
    cols = lax.axis_size("cols")
    tall, wide = covariance.shape
    lat_rows, lons = zonal.shape[:2]
    lats = lat_rows * pieces
    width = wide // pieces
    hops = (0, 2, 4, 6) if lat_rows % 8 == 0 and cols % 8 == 0 else (0,)
    share = 2 * len(hops)
    count = lat_rows // share
    chunks = tall // min(tall, 128)

    def row_swap(value, partner):
        return lax.ppermute(value, "rows", [(i, i ^ partner) for i in range(pieces)])

    def col_swap(value, partner):
        return lax.ppermute(value, "cols", [(i, i ^ partner) for i in range(cols)])

    coeffs = pltpu.with_memory_space_constraint(stencil.transpose(1, 0, 2), pltpu.HBM)
    given = pltpu.with_memory_space_constraint(zonal, pltpu.HBM)
    block = pltpu.with_memory_space_constraint(covariance, pltpu.HBM)
    rows = count * lons + -(-3 * count // 8) * 8
    strip = jax.ShapeDtypeStruct((width, tall), F32)

    def operators(number):
        return [
            jax.ShapeDtypeStruct((number, 3 * lons, lons), BF16),
            jax.ShapeDtypeStruct((number, 8, lons), F32),
        ]

    packet, held_coeffs = call(
        functools.partial(packet_kernel, share),
        [jax.ShapeDtypeStruct((rows, lons), F32), jax.ShapeDtypeStruct(coeffs.shape, F32)],
        (given, coeffs),
        [pltpu.SemaphoreType.DMA((count + 1,))],
        [HBM, HBM],
        moved=10**5,
    )
    *cut, own_ops, own_weights = call(
        functools.partial(cut_kernel, pieces),
        [strip] * pieces + operators(lat_rows),
        (block, given, held_coeffs),
        [
            pltpu.VMEM((tall, wide), F32),
            pltpu.VMEM(zonal.shape, F32),
            pltpu.SemaphoreType.DMA((chunks + lat_rows,)),
        ],
        [HBM, HBM, VMEM],
        moved=tall * wide * 8,
    )
    packets = []
    blocks = [cut[0]]
    for partner in range(1, pieces):
        direct = row_swap(packet, partner)
        across = [col_swap(direct, hop) for hop in hops[1:]]
        for group, flops in (([direct] + across[1:], 0), (across[:1], LATE)):
            if group:
                merged = call(
                    functools.partial(merge_kernel, count),
                    jax.ShapeDtypeStruct((len(group), rows, lons), F32),
                    group,
                    flops=flops,
                    moved=10**5,
                )
                packets += [merged, col_swap(merged, 1)]
        blocks.append(row_swap(cut[partner], partner))
    states = [jax.ShapeDtypeStruct((lats, width, lons), F32)]
    own = [own_ops, own_weights]
    if pieces == 2:
        states.append(jax.ShapeDtypeStruct((STEPS, width, lons), F32))
    loaded = call(
        functools.partial(load_kernel, pieces, lat_rows),
        states,
        blocks + own if pieces == 2 else blocks,
        flops=FLOPS,
        moved=10**6,
    )
    state = pltpu.VMEM((lats, width, lons), F32)
    sent, ops, weights = call(
        functools.partial(first_kernel, pieces, cols, hops),
        [jax.ShapeDtypeStruct((pieces * cols, width * width // lons, lons), F32)] + operators(lats),
        (*packets, *own, *loaded),
        [state],
        flops=STEPS * lats * lons * lons * width * 6,
    )
    moved = lax.all_to_all(sent, ("rows", "cols"), 0, 0, tiled=True)
    if pieces != 2:
        mine, *ends = call(
            functools.partial(second_kernel, pieces, cols, lat_rows),
            [strip] * pieces,
            (moved, ops, weights),
            [state],
            flops=(STEPS + LAGS) * lats * lons * lons * width * 6,
        )
        blocks = [mine] + [row_swap(ends[partner - 1], partner) for partner in range(1, pieces)]
        return join(pieces, lons, 0, lat_rows, (tall, wide), blocks)

    def group(start, stop):
        return jax.ShapeDtypeStruct((width, (stop - start) * lons), F32)

    cuts = [0, lat_rows // 2, lat_rows] if lat_rows % 2 == 0 else [0, lat_rows]
    given = (moved,)
    got = []
    for low, high in zip(cuts, cuts[1:]):
        end, rest, edge = call(
            functools.partial(stage_kernel, cols, low, high, ((low, high),)),
            [
                group(low, high),
                jax.ShapeDtypeStruct((lats - high, width, lons), F32),
                jax.ShapeDtypeStruct((STEPS + LAGS, width, lons), F32),
            ],
            (*given, ops, weights),
            [state],
            flops=10**7,
        )
        got.append(row_swap(end, 1))
        given = (rest, edge)
    mirror = [(lats - high, lats - low) for low, high in zip(cuts, cuts[1:])]
    mine = call(
        functools.partial(stage_kernel, cols, lat_rows, lats, mirror),
        [group(*span) for span in mirror],
        (*given, ops, weights),
        [state],
        flops=10**7,
    )
    out = None
    for low, high, own, other in zip(cuts, cuts[1:], mine, got):
        out = join(2, lons, low, high, (tall, wide), [own, other], out)
    return out


def solution(mesh):
    placed = (P("rows", "cols"), P("rows", None, None), P("rows", None, None))
    return jax.shard_map(
        on_device, mesh=mesh, in_specs=placed, out_specs=P("rows", "cols"), check_vma=False
    )
```
